128 devices in a mesh: row: 8 (over x, y_lo), col: 16 (over y_hi, z, core).
Axes of the slice: x: 4, y: 4 (y_hi: 2, y_lo: 2; y = y_hi * 2 + y_lo), z: 4, core: 2. Of those that a mesh axis runs over, the one named last changes fastest.
Arguments:
- front: float32 [10240, 10240], P('row', 'col'), as said below
- updates: float32 [16384, 8192], P('row', 'col'), as said below
- maps: int32 [2, 64], replicated, may hold values from 0 to 79, as said below
Outputs:
- panel_factor: float32 [10240, 2048], P('row', 'col')
- trailing: float32 [10240, 10240], P('row', 'col')
The draws below stay inside these ranges and needn't reach their ends.
Inputs may be any that keep to these rules, and one draw needn't show every extreme that they name: `maps`: each row lists 64 distinct front blocks; entry j leaves remainder floor(j / 4) on division by 16, the entries of one remainder rise with j, and blocks 0 and 79 appear in both rows. Symmetric in front order; the assembled leading 2048 x 2048 block is positive definite. `updates`: each child's update is symmetric in the child's own order.
All inputs are finite; a program needn't handle non-finite values.
Results may differ from the reference program's by a relative error of at most 0.0001.
Values sent between devices are 32-bit elements; how exact they have to be, the bound alone decides.
No kernel may reach another device: no remote copies, remote signals or barrier semaphores. Data moves between devices by JAX's collectives and lax.ppermute only.
A program may use at most 192 MiB of HBM per device.

```python
import math
import jax
import jax.numpy as jnp
from jax import lax

BLK = 128
NF = 10240
NC = 8192
PW = 2048
NB = 80
NCB = 64
ROW_DEVS = 8
COLUMN_DEVS = 16
CGRP = 4


spread = 0.06


def to_stored_drawn(matrix, parts):
    per_part = matrix.shape[0] // BLK // parts
    return matrix.reshape(per_part, parts, BLK, -1).transpose(1, 0, 2, 3).reshape(matrix.shape)


def symmetric_part(key, order):
    base = jax.random.normal(key, (order, order), jnp.float32) * spread
    return (base + base.T) * math.sqrt(0.5)


def draw_front(key, part):
    first_key, second_key = jax.random.split(key)
    sym = symmetric_part(first_key, NF)
    diagonal = 12.0 * (1.0 + jax.random.uniform(second_key, (NF,), jnp.float32))
    index = jnp.arange(NF)
    full = sym + jnp.where(index[:, None] == index[None, :], diagonal[:, None], jnp.float32(0.0))
    return to_stored_drawn(to_stored_drawn(full, ROW_DEVS).T, COLUMN_DEVS).T


def draw_updates(key, part):
    children = []
    for which_child in range(2):
        child_key = jax.random.fold_in(key, 11 + which_child)
        sym = symmetric_part(child_key, NC)
        children.append(to_stored_drawn(sym, ROW_DEVS // 2))
    return jnp.concatenate(children, axis=0)


def draw_maps(key, part):
    slots = NB // COLUMN_DEVS

    def one_group(which_child, column):
        group_key = jax.random.fold_in(jax.random.fold_in(key, 7), which_child * COLUMN_DEVS + column)
        scores = jax.random.permutation(group_key, slots).astype(jnp.int32)
        forced = jnp.where(column == 0, 0, jnp.where(column == COLUMN_DEVS - 1, slots - 1, -5))
        scores = jnp.where(jnp.arange(slots) == forced, -1, scores)
        chosen = jnp.sort(jnp.argsort(scores)[:CGRP]).astype(jnp.int32)
        return chosen * COLUMN_DEVS + column
    columns = jnp.arange(COLUMN_DEVS, dtype=jnp.int32)
    children = jnp.arange(2, dtype=jnp.int32)
    table = jax.vmap(lambda child_at: jax.vmap(lambda col_now: one_group(child_at, col_now))(columns))(children)
    return table.reshape(2, NCB).astype(jnp.int32)


def setup_inputs(seed: int = 0) -> dict:
    key_of = jax.random.split(jax.random.key(seed), 4)
    front = draw_front(jax.random.fold_in(key_of[3], 71), 0)
    updates = draw_updates(jax.random.fold_in(key_of[3], 71), 0)
    maps = draw_maps(jax.random.fold_in(key_of[3], 71), 0)
    return {"front": front, "updates": updates, "maps": maps}


def to_front(matrix, parts):
    per_part = matrix.shape[0] // BLK // parts
    return matrix.reshape(parts, per_part, BLK, -1).transpose(1, 0, 2, 3).reshape(matrix.shape)

def to_stored(matrix, parts):
    per_part = matrix.shape[0] // BLK // parts
    return matrix.reshape(per_part, parts, BLK, -1).transpose(1, 0, 2, 3).reshape(matrix.shape)

def embed_child(child_matrix, child_map):
    onehot = (child_map[None, :] == jnp.arange(NB, dtype=jnp.int32)[:, None]).astype(jnp.float32)
    child_blocks = child_matrix.reshape(NCB, BLK, NCB, BLK)
    placed = jnp.einsum('pi,iajb->pajb', onehot, child_blocks, precision=lax.Precision.HIGHEST)
    placed = jnp.einsum('pajb,qj->paqb', placed, onehot, precision=lax.Precision.HIGHEST)
    return placed.reshape(NF, NF)

def reference(front, updates, maps):
    front0 = to_front(to_front(front, ROW_DEVS).T, COLUMN_DEVS).T
    assembled = front0
    for which_child in range(2):
        child_part = updates[which_child * NC:(which_child + 1) * NC]
        child_matrix = to_front(child_part, ROW_DEVS // 2)
        assembled = assembled + embed_child(child_matrix, maps[which_child])
    factor11 = jnp.linalg.cholesky(assembled[:PW, :PW])
    factor21 = jax.scipy.linalg.solve_triangular(factor11, assembled[PW:, :PW].T, lower=True).T
    panel = jnp.concatenate([factor11, factor21], axis=0)
    product = jnp.dot(panel.astype(jnp.float32), panel.T.astype(jnp.float32), precision=lax.Precision.HIGHEST, preferred_element_type=jnp.float32)
    keep = jnp.arange(NF) >= PW
    trailing = jnp.where(keep[:, None] & keep[None, :], assembled - product, jnp.float32(0.0))
    panel_out = to_stored(to_stored(panel, ROW_DEVS).T, COLUMN_DEVS).T
    trailing_out = to_stored(to_stored(trailing, ROW_DEVS).T, COLUMN_DEVS).T
    return (panel_out, trailing_out)
```

```python
import functools

import jax
import jax.numpy as jnp
from jax import lax
from jax.experimental import pallas as pl
from jax.experimental.pallas import tpu as pltpu
from jax.sharding import PartitionSpec as P

BLK = 128
PW = 2048
STRIP = 512
STEP = 256
CALLS = PW // STRIP
BOTH = ("row", "col")
OFFSETS = (0, -1, 1, 2)
F32 = jnp.float32
BF16 = jnp.bfloat16
PARAMS = pltpu.CompilerParams(vmem_limit_bytes=58 << 20)
ANY = pl.BlockSpec(memory_space=pl.ANY)
VMEM = pl.BlockSpec(memory_space=pltpu.VMEM)
SMEM = pl.BlockSpec(memory_space=pltpu.SMEM)


def flat(x, y, z, core):
    return ((x % 4) * 2 + y % 2) * 16 + ((y % 4) // 2) * 8 + (z % 4) * 2 + core % 2


def shift(dx=0, dy=0, dz=0, dcore=0):
    every = [(x, y, z, c) for x in range(4) for y in range(4) for z in range(4) for c in range(2)]
    return [(flat(x, y, z, c), flat(x + dx, y + dy, z + dz, c + dcore)) for x, y, z, c in every]


def move(value, **by):
    return lax.ppermute(value, BOTH, shift(**by))


def ring(block, axis):
    half = block.shape[0] // 2
    below = move(block, **{axis: 1})
    above = move(block, **{axis: -1})
    first = move(below[:half], **{axis: 1})
    second = move(above[half:], **{axis: -1})
    return below, above, first, second


def gather_leading(corner):
    pair = corner.reshape(2, BLK, BLK)
    below, above, first, second = ring(pair, "dy")
    upper = jnp.stack([pair[0], below[0], above[0], first[0]])
    lower = jnp.stack([pair[1], below[1], above[1], second[0]])
    pieces = []
    for block, one, other in ((upper, "dz", "dx"), (lower, "dx", "dz")):
        below, above, first, second = ring(block, one)
        group = jnp.stack([block, below, above, jnp.concatenate([first, second])])
        mine = [group, *ring(group, other)]
        pieces += [mine, [move(piece, dcore=1) for piece in mine]]
    return pieces


def eliminate(tiles):
    tiles = list(tiles)
    count = len(tiles)
    lane = lax.broadcasted_iota(jnp.int32, (8, BLK), 1)
    sub = lax.broadcasted_iota(jnp.int32, (8, BLK), 0)
    upper = []

    def by_lane(x, j):
        return jnp.broadcast_to(x[:, j : j + 1], (8, BLK))

    def by_sub(x, s):
        return jnp.broadcast_to(x[s : s + 1, :], (8, BLK))

    for p in range(count):
        now = tiles[p]
        o = 8 * p
        inside = (lane >= o) & (lane < o + 8)
        column = [by_lane(now, o + t) for t in range(8)]
        a = {(s, t): by_sub(column[t], s) for t in range(8) for s in range(t, 8)}
        rows = [by_sub(now, t) for t in range(8)]
        unit = [jnp.where(lane == o + t, F32(1), jnp.where(inside, F32(0), rows[t])) for t in range(8)]
        r = []
        low = {}
        for t in range(8):
            r.append(lax.rsqrt(a[t, t]))
            for s in range(t + 1, 8):
                low[s, t] = a[s, t] * r[t]
            for u in range(t + 1, 8):
                for s in range(u, 8):
                    a[s, u] = a[s, u] - low[s, t] * low[u, t]
        z = []
        q = []
        for t in range(8):
            z_now, q_now = unit[t], rows[t]
            for s in range(t):
                z_now = z_now - low[t, s] * z[s]
                q_now = q_now - low[t, s] * q[s]
            z.append(z_now * r[t])
            q.append(q_now * r[t])
        y = [None] * 8
        for t in reversed(range(8)):
            y_now = z[t]
            for s in range(t + 1, 8):
                y_now = y_now - low[s, t] * y[s]
            y[t] = y_now * r[t]
        z_tile, q_tile = z[0], q[0]
        for t in range(1, 8):
            z_tile = jnp.where(sub == t, z[t], z_tile)
            q_tile = jnp.where(sub == t, q[t], q_tile)
        upper.append(jnp.where(lane >= o + sub, q_tile, F32(0)))
        tiles[p] = jnp.where(lane <= o + sub, z_tile, F32(0))
        for i in range(p + 1, count):
            terms = [by_lane(tiles[i], o + t) * y[t] for t in range(8)]
            while len(terms) > 1:
                terms = [terms[k] + terms[k + 1] for k in range(0, len(terms), 2)]
            tiles[i] = jnp.where(inside, F32(0), tiles[i]) - terms[0]
    return tiles, upper


def split(x):
    high = x.astype(BF16)
    return high, (x - high.astype(F32)).astype(BF16)


def dot_nt(a, b):
    return lax.dot_general(a, b, (((1,), (1,)), ((), ())), preferred_element_type=F32)


def dot_nn(a, b):
    return lax.dot_general(a, b, (((1,), (0,)), ((), ())), preferred_element_type=F32)


def pairs(dot, ah, al, bh, bl):
    return dot(ah, bh) + (dot(ah, bl) + dot(al, bh))


def exact_nt(a, b):
    return lax.dot_general(a, b, (((1,), (1,)), ((), ())), precision=lax.Precision.HIGHEST, preferred_element_type=F32)


def exact_nn(a, b):
    return jnp.dot(a, b, precision=lax.Precision.HIGHEST, preferred_element_type=F32)


def offset_of(index):
    return jnp.where(index == 3, 2, jnp.where(index == 2, 1, jnp.where(index == 1, -1, 0)))


def load_leading(place, pieces, dest, sem, first_col, cols):
    x, y, z, core = place[0], place[1], place[2], place[3]
    for half in range(2):
        for swapped in range(2):
            for piece in range(5):
                ref = pieces[(half * 2 + swapped) * 5 + piece]
                wide = ref.shape[0]
                base = 2 if piece == 4 else 0
                far = (0, -1, 1, 2, 2)[piece]

                def one(n, carry, ref=ref, base=base, far=far, half=half, swapped=swapped):
                    i, dy = n // 4, n % 4
                    near = offset_of(i + base)
                    dx, dz = (far, near) if half == 0 else (near, far)
                    xs, ys, zs = (x + dx + 4) % 4, (y + offset_of(dy) + 4) % 4, (z + dz + 4) % 4
                    cs = (core + swapped) % 2
                    block_row = xs * 2 + ys % 2 + 8 * half
                    block_col = (ys // 2) * 8 + zs * 2 + cs - first_col

                    @pl.when((block_col >= 0) & (block_col < cols))
                    def _():
                        pltpu.make_async_copy(
                            ref.at[i, dy],
                            dest.at[block_col, pl.ds(pl.multiple_of(block_row * BLK, BLK), BLK), :],
                            sem,
                        ).start()

                    return carry

                lax.fori_loop(0, wide * 4, one, 0)


def factor_kernel(call, place, *refs):
    pieces = refs[:20]
    earlier = refs[20 : 20 + 2 * call]
    out_high, out_low, inv_high, inv_low = refs[20 + 2 * call : 24 + 2 * call]
    (lead, high, low, c, diag, inverse, upper, inverse1, low21, load_sem, strip_sem, out_sem) = refs[24 + 2 * call :]
    start = STRIP * call
    load_leading(place, pieces, lead, load_sem, 4 * call, 4)
    copies = []
    for n in range(call):
        for which, dest in ((0, high), (1, low)):
            copies.append(
                pltpu.make_async_copy(
                    earlier[2 * n + which].at[pl.ds(start - STRIP * n, PW - start), :],
                    dest.at[:, pl.ds(STRIP * n, STRIP)],
                    strip_sem.at[2 * n + which],
                )
            )
    for copy in copies:
        copy.start()
    pltpu.make_async_copy(lead, lead, load_sem).wait()
    for copy in copies:
        copy.wait()

    def put(rows, cols, value):
        h, l = split(value)
        high[rows, cols] = h
        low[rows, cols] = l

    def before(kk):
        known = start + STEP * kk
        r0 = STEP * kk
        tiles = (PW - start - r0) // STEP

        def tile(t, carry):
            at = pl.multiple_of(r0 + t * STEP, STEP)
            rows = pl.ds(at, STEP)
            whole = pl.ds(pl.multiple_of(start + at, STEP), STEP)
            value = jnp.concatenate([lead[2 * kk, whole, :], lead[2 * kk + 1, whole, :]], axis=1)
            if known > 0:
                value = value - pairs(
                    dot_nt, high[rows, :known], low[rows, :known], high[r0 : r0 + STEP, :known], low[r0 : r0 + STEP, :known]
                )
            c[rows, :] = value
            return carry

        lax.fori_loop(0, tiles, tile, 0)
        diag[...] = c[r0 : r0 + BLK, :BLK]

    def between(kk):
        r0 = STEP * kk
        col = start + r0
        w1 = inverse[...]
        l21 = exact_nt(c[r0 + BLK : r0 + STEP, :BLK], w1)
        diag[...] = c[r0 + BLK : r0 + STEP, BLK:] - exact_nt(l21, l21)
        inverse1[...] = w1
        low21[...] = l21
        put(pl.ds(r0, BLK), pl.ds(col, BLK), upper[...].T)
        put(pl.ds(r0, BLK), pl.ds(col + BLK, BLK), jnp.zeros((BLK, BLK), F32))
        put(pl.ds(r0 + BLK, BLK), pl.ds(col, BLK), l21)

    def after(kk):
        r0 = STEP * kk
        col = start + r0
        w2 = inverse[...]
        put(pl.ds(r0 + BLK, BLK), pl.ds(col + BLK, BLK), upper[...].T)
        w21 = -exact_nn(w2, exact_nn(low21[...], inverse1[...]))
        top = jnp.concatenate([inverse1[...], jnp.zeros((BLK, BLK), F32)], axis=1)
        w = jnp.concatenate([top, jnp.concatenate([w21, w2], axis=1)], axis=0)
        wh, wl = split(w)
        inv_high[kk] = wh
        inv_low[kk] = wl
        tiles = (PW - start - r0) // STEP

        def tile(t, carry):
            rows = pl.ds(pl.multiple_of(r0 + t * STEP, STEP), STEP)
            ch, cl = split(c[rows, :])
            put(rows, pl.ds(col, STEP), pairs(dot_nt, ch, cl, inv_high[kk], inv_low[kk]))
            return carry

        lax.fori_loop(1, tiles, tile, 0)

    def half(h, carry):
        for kk in range(STRIP // STEP):
            pl.when(h == 2 * kk)(functools.partial(before, kk))
        w, u = eliminate([diag[8 * i : 8 * i + 8, :] for i in range(16)])
        for i in range(16):
            inverse[8 * i : 8 * i + 8, :] = w[i]
            upper[8 * i : 8 * i + 8, :] = u[i]
        for kk in range(STRIP // STEP):
            pl.when(h == 2 * kk)(functools.partial(between, kk))
            pl.when(h == 2 * kk + 1)(functools.partial(after, kk))
        return carry

    lax.fori_loop(0, STRIP // BLK, half, 0)
    outs = [
        pltpu.make_async_copy(high.at[:, pl.ds(start, STRIP)], out_high, out_sem.at[0]),
        pltpu.make_async_copy(low.at[:, pl.ds(start, STRIP)], out_low, out_sem.at[1]),
    ]
    for copy in outs:
        copy.start()
    for copy in outs:
        copy.wait()


def factor_strip(call, place, pieces, earlier):
    rows = PW - STRIP * call
    known = STRIP * (call + 1)
    strip = jax.ShapeDtypeStruct((rows, STRIP), BF16)
    inverses = jax.ShapeDtypeStruct((STRIP // STEP, STEP, STEP), BF16)
    block = pltpu.VMEM((BLK, BLK), F32)
    return pl.pallas_call(
        functools.partial(factor_kernel, call),
        out_shape=[strip, strip, inverses, inverses],
        in_specs=[SMEM] + [ANY] * (20 + 2 * call),
        out_specs=[ANY, ANY, VMEM, VMEM],
        scratch_shapes=[
            pltpu.VMEM((4, PW, BLK), F32),
            pltpu.VMEM((rows, known), BF16),
            pltpu.VMEM((rows, known), BF16),
            pltpu.VMEM((rows, STEP), F32),
            block,
            block,
            block,
            block,
            block,
            pltpu.SemaphoreType.DMA,
            pltpu.SemaphoreType.DMA((max(2 * call, 1),)),
            pltpu.SemaphoreType.DMA((2,)),
        ],
        compiler_params=PARAMS,
        name=f"factor{call}",
    )(place, *pieces, *earlier)


def assemble_kernel(source, valid, colsel, front, f0, f1, g0, g1, out):
    q = pl.program_id(0)
    del source
    out[:, :BLK] = front[:, :BLK]
    for n in range(5):
        cols = slice(n * BLK, (n + 1) * BLK)
        total = front[:, cols]
        for child, (first, rest) in enumerate(((f0, g0), (f1, g1))):
            use = valid[child, q]
            sel = colsel[child, n]

            def block(j, first=first, rest=rest):
                return first[0, 0] if j == 0 else rest[0, 0, :, (j - 1) * BLK : j * BLK]

            if n < 4:
                total = total + jnp.where((sel == 1) & (use == 1), block(n), F32(0))
            if n > 0:
                total = total + jnp.where((sel == 2) & (use == 1), block(n - 1), F32(0))
        out[:, cols] = total


def assemble(source, valid, colsel, front, first, rest):
    def pick(child):
        return lambda q, s, v, c: (q % 2, s[child, q], 0, 0)

    rows, cols = front.shape
    return pl.pallas_call(
        assemble_kernel,
        out_shape=jax.ShapeDtypeStruct(front.shape, F32),
        grid_spec=pltpu.PrefetchScalarGridSpec(
            num_scalar_prefetch=3,
            grid=(rows // BLK,),
            in_specs=[
                pl.BlockSpec((BLK, cols), lambda q, *_: (q, 0)),
                pl.BlockSpec((1, 1, BLK, BLK), pick(0)),
                pl.BlockSpec((1, 1, BLK, BLK), pick(1)),
                pl.BlockSpec((1, 1, BLK, 3 * BLK), pick(0)),
                pl.BlockSpec((1, 1, BLK, 3 * BLK), pick(1)),
            ],
            out_specs=pl.BlockSpec((BLK, cols), lambda q, *_: (q, 0)),
        ),
        compiler_params=PARAMS,
        name="assemble",
    )(source, valid, colsel, front, first, first, rest, rest)


def solve_kernel(place, *refs):
    strips, inverses, slabs = refs[:8], refs[8:16], refs[16:24]
    panel_rows, asm, panel_out, trailing = refs[24:28]
    high, low, xh, xl, yh, yl, raw, yraw, sems, raw_sem, slab_sem = refs[28:]
    x, y, z, core = place[0], place[1], place[2], place[3]
    row = x * 2 + y % 2
    col = (y // 2) * 8 + z * 2 + core
    wait_strip = []
    for n in range(CALLS):
        for which, dest in ((0, high), (1, low)):
            copy = pltpu.make_async_copy(
                strips[2 * n + which],
                dest.at[pl.ds(STRIP * n, PW - STRIP * n), pl.ds(STRIP * n, STRIP)],
                sems.at[2 * n + which],
            )
            wait_strip.append(copy)
    raws = [pltpu.make_async_copy(panel_rows.at[pl.ds(4 * n, 4)], raw.at[pl.ds(4 * n, 4)], raw_sem.at[n]) for n in range(4)]
    slab_copies = []
    for dx in range(4):
        for dl in range(2):
            there = ((x + dx) % 4) * 2 + (y + dl) % 2
            for second in range(2):
                at = pl.multiple_of((there + 8 * second) * BLK, BLK)
                slab_copies.append(
                    pltpu.make_async_copy(
                        slabs[dx * 2 + dl].at[pl.ds(second * BLK, BLK), :],
                        yraw.at[pl.ds(at, BLK), :],
                        slab_sem.at[(dx * 2 + dl) * 2 + second],
                    )
                )
    raws[0].start()
    for copy in slab_copies:
        copy.start()
    for n in range(CALLS):
        wait_strip[2 * n].start()
        wait_strip[2 * n + 1].start()
        if n:
            raws[n].start()
    for copy in slab_copies:
        copy.wait()
    panel_out[: 2 * BLK, :] = jnp.zeros((2 * BLK, BLK), F32)
    for k in range(PW // STEP):
        known = STEP * k
        if k % 2 == 0:
            raws[k // 2].wait()
            wait_strip[k].wait()
            wait_strip[k + 1].wait()
        wh, wl = inverses[2 * (k // 2)], inverses[2 * (k // 2) + 1]
        here = slice(known, known + STEP)
        value = yraw[here, :]
        if k:
            value = value - pairs(dot_nn, high[here, :known], low[here, :known], yh[:known, :], yl[:known, :])
        vh, vl = split(value)
        got = pairs(dot_nn, wh[k % 2], wl[k % 2], vh, vl)
        yh[here, :], yl[here, :] = split(got)

        def tile(t, carry, k=k, known=known, here=here, wh=wh, wl=wl):
            rows = pl.ds(pl.multiple_of(t * STEP, STEP), STEP)
            value = jnp.concatenate([raw[2 * k, rows, :], raw[2 * k + 1, rows, :]], axis=1)
            if k:
                value = value - pairs(dot_nt, xh[rows, :known], xl[rows, :known], high[here, :known], low[here, :known])
            vh, vl = split(value)
            got = pairs(dot_nt, vh, vl, wh[k % 2], wl[k % 2])
            xh[rows, here], xl[rows, here] = split(got)
            for side in range(2):

                @pl.when(col == 2 * k + side)
                def _():
                    panel_out[pl.ds(pl.multiple_of(2 * BLK + t * STEP, BLK), STEP), :] = got[:, side * BLK : (side + 1) * BLK]

            return carry

        lax.fori_loop(0, raw.shape[1] // STEP, tile, 0)
    lanes = pl.ds(pl.multiple_of(col * BLK, BLK), BLK)
    for second in range(2):
        block_row = row + 8 * second

        @pl.when(block_row >= col)
        def _():
            rows = pl.ds(pl.multiple_of(block_row * BLK, BLK), BLK)
            panel_out[second * BLK : (second + 1) * BLK, :] = high[rows, lanes].astype(F32) + low[rows, lanes].astype(F32)

    trailing[: 2 * BLK, :] = jnp.zeros((2 * BLK, trailing.shape[1]), F32)
    trailing[:, :BLK] = jnp.zeros((trailing.shape[0], BLK), F32)

    def update(t, carry):
        rows = pl.ds(pl.multiple_of(t * STEP, STEP), STEP)
        out = pl.ds(pl.multiple_of(2 * BLK + t * STEP, STEP), STEP)
        trailing[out, BLK:] = asm[out, BLK:] - pairs(dot_nn, xh[rows, :], xl[rows, :], yh[...], yl[...])
        return carry

    lax.fori_loop(0, raw.shape[1] // STEP, update, 0)


def solve(place, strips, inverses, slabs, panel_rows, asm):
    rows, cols = asm.shape
    under = rows - 2 * BLK
    return pl.pallas_call(
        solve_kernel,
        out_shape=[jax.ShapeDtypeStruct((rows, BLK), F32), jax.ShapeDtypeStruct((rows, cols), F32)],
        in_specs=[SMEM] + [ANY] * 8 + [VMEM] * 8 + [ANY] * 9 + [VMEM],
        out_specs=[VMEM, VMEM],
        scratch_shapes=[
            pltpu.VMEM((PW, PW), BF16),
            pltpu.VMEM((PW, PW), BF16),
            pltpu.VMEM((under, PW), BF16),
            pltpu.VMEM((under, PW), BF16),
            pltpu.VMEM((PW, cols - BLK), BF16),
            pltpu.VMEM((PW, cols - BLK), BF16),
            pltpu.VMEM((16, under, BLK), F32),
            pltpu.VMEM((PW, cols - BLK), F32),
            pltpu.SemaphoreType.DMA((8,)),
            pltpu.SemaphoreType.DMA((4,)),
            pltpu.SemaphoreType.DMA((16,)),
        ],
        compiler_params=PARAMS,
        name="solve",
    )(place, *strips, *inverses, *slabs, panel_rows, asm)


def local(front, updates, maps):
    row_at = lax.axis_index("row")
    col_at = lax.axis_index("col")
    place = jnp.stack([row_at // 2, (col_at // 8) * 2 + row_at % 2, (col_at // 2) % 4, col_at % 2]).astype(jnp.int32)
    slots = maps >> 4
    row_slots = lax.dynamic_index_in_dim(slots.reshape(2, 2, 8, 4), row_at, 2, keepdims=False)
    col_slots = lax.dynamic_index_in_dim(slots.reshape(2, 16, 4), col_at, 1, keepdims=False)

    first = lax.all_to_all(updates[:, :BLK].reshape(2, 8, BLK, BLK), "row", split_axis=1, concat_axis=1, tiled=True)
    meets = col_slots[:, 0] == 0
    panel = front[:, :BLK].reshape(5, 2, BLK, BLK)
    parts = []
    for m in range(5):
        total = panel[m]
        for child in range(2):
            for a in (m, m - 1):
                if 0 <= a < 4:
                    hit = (row_slots[child, :, a] == m) & meets[child]
                    total = total + jnp.where(hit[:, None, None], first[:, 4 * child + a], F32(0))
        parts.append(total)
    corner = parts[0].reshape(2 * BLK, BLK)
    under = jnp.stack(parts[1:]).reshape(8 * BLK, BLK)
    pieces = gather_leading(corner)
    flat_pieces = [piece for group in pieces for piece in group]

    last = flat_pieces[1][0, 0, :8]
    under, others, last = lax.optimization_barrier((under, updates[:, BLK:], last))
    panel_rows = lax.all_gather(under, "col", axis=0, tiled=True).reshape(16, 8 * BLK, BLK)
    rest = lax.all_to_all(others.reshape(2, 8, BLK, 3 * BLK), "row", split_axis=1, concat_axis=1, tiled=True)

    strips, inverses = [], []
    got = factor_strip(0, place, flat_pieces, [])
    strips += got[:2]
    inverses += got[2:]

    slot = jnp.arange(5)
    own = jnp.pad(row_slots, ((0, 0), (0, 0), (0, 1)), constant_values=-1) == slot
    prior = jnp.pad(row_slots, ((0, 0), (0, 0), (1, 0)), constant_values=-1) == slot
    valid = (own | prior).astype(jnp.int32)
    source = jnp.where(own, slot, jnp.where(prior, slot - 1, 0)) + 4 * jnp.arange(2)[:, None, None]
    valid = valid.transpose(0, 2, 1).reshape(2, 10)
    source = source.transpose(0, 2, 1).reshape(2, 10).astype(jnp.int32)
    own = jnp.pad(col_slots, ((0, 0), (0, 1)), constant_values=-1) == slot
    prior = jnp.pad(col_slots, ((0, 0), (1, 0)), constant_values=-1) == slot
    colsel = jnp.where(own, 1, jnp.where(prior, 2, 0)).astype(jnp.int32)
    asm = assemble(source, valid, colsel, front, first, rest)
    head = asm[: 2 * BLK, BLK:]
    slabs = []
    for dx in range(4):
        for dl in range(2):
            if dx == 0 and dl == 0:
                slabs.append(head)
                continue
            there = [(r, ((r // 2 - dx) % 4) * 2 + (r + dl) % 2) for r in range(8)]
            slabs.append(lax.ppermute(head, "row", there))
    for call in range(1, CALLS):
        got = factor_strip(call, place, flat_pieces, strips)
        strips += got[:2]
        inverses += got[2:]
    return tuple(solve(place, strips, inverses, slabs, panel_rows, asm))


def solution(mesh):
    in_specs = (P("row", "col"), P("row", "col"), P())
    out_specs = (P("row", "col"), P("row", "col"))
    return jax.shard_map(local, mesh=mesh, in_specs=in_specs, out_specs=out_specs, check_vma=False)
```

```python
import functools

import jax
import jax.numpy as jnp
from jax import lax
from jax.experimental import pallas as pl
from jax.experimental.pallas import tpu as pltpu
from jax.sharding import PartitionSpec as P

BLK = 128
PW = 2048
STRIP = 512
STEP = 256
CALLS = PW // STRIP
BOTH = ("row", "col")
OFFSETS = (0, -1, 1, 2)
NEAR = 2
F32 = jnp.float32
BF16 = jnp.bfloat16
PARAMS = pltpu.CompilerParams(vmem_limit_bytes=58 << 20)
ANY = pl.BlockSpec(memory_space=pl.ANY)
VMEM = pl.BlockSpec(memory_space=pltpu.VMEM)
SMEM = pl.BlockSpec(memory_space=pltpu.SMEM)


def flat(x, y, z, core):
    return ((x % 4) * 2 + y % 2) * 16 + ((y % 4) // 2) * 8 + (z % 4) * 2 + core % 2


def shift(dx=0, dy=0, dz=0, dcore=0):
    every = [(x, y, z, c) for x in range(4) for y in range(4) for z in range(4) for c in range(2)]
    return [(flat(x, y, z, c), flat(x + dx, y + dy, z + dz, c + dcore)) for x, y, z, c in every]


def move(value, **by):
    return lax.ppermute(value, BOTH, shift(**by))


def ring(block, axis):
    half = block.shape[0] // 2
    below = move(block, **{axis: 1})
    above = move(block, **{axis: -1})
    first = move(below[:half], **{axis: 1})
    second = move(above[half:], **{axis: -1})
    return below, above, first, second


def settled(value, *tokens):
    ready = functools.reduce(jnp.logical_and, [token <= F32(jnp.finfo(jnp.float32).max) for token in tokens])
    return jnp.where(ready, value, jnp.zeros((), value.dtype))


def gather_leading(corner, y_at):
    pair = corner.reshape(2, BLK, BLK)
    below, above, first, second = ring(pair, "dy")

    def in_order(half, opposite, wanted):
        blocks = []
        for y in wanted:
            d = (y - y_at) & 3
            blocks.append(
                jnp.where(d == 0, pair[half], jnp.where(d == 1, above[half], jnp.where(d == 2, opposite, below[half])))
            )
        return jnp.stack(blocks)

    upper = in_order(0, first[0], (0, 1))
    lower = in_order(1, second[0], (0, 1))
    late = in_order(1, second[0], (2, 3))
    pieces = []
    for block, one, other in ((upper, "dz", "dx"), (lower, "dx", "dz")):
        below, above, first, second = ring(block, one)
        group = jnp.stack([block, below, above, jnp.concatenate([first, second])])
        mine = [group, *ring(group, other)]
        pieces += [*mine, *[move(piece, dcore=1) for piece in mine]]
    below, above, first, second = ring(late, "dz")
    late = jnp.stack([late, below, above, jnp.concatenate([first, second])])
    return pieces, late


def along_x(late):
    return late, move(late, dx=1), move(late, dx=-1), move(late, dx=2)


def eliminate(tiles):
    tiles = list(tiles)
    count = len(tiles)
    lane = lax.broadcasted_iota(jnp.int32, (8, BLK), 1)
    sub = lax.broadcasted_iota(jnp.int32, (8, BLK), 0)
    upper = []

    def by_lane(x, j):
        return jnp.broadcast_to(x[:, j : j + 1], (8, BLK))

    def by_sub(x, s):
        return jnp.broadcast_to(x[s : s + 1, :], (8, BLK))

    for p in range(count):
        now = tiles[p]
        o = 8 * p
        inside = (lane >= o) & (lane < o + 8)
        column = [by_lane(now, o + t) for t in range(8)]
        a = {(s, t): by_sub(column[t], s) for t in range(8) for s in range(t, 8)}
        rows = [by_sub(now, t) for t in range(8)]
        unit = [jnp.where(lane == o + t, F32(1), jnp.where(inside, F32(0), rows[t])) for t in range(8)]
        r = []
        low = {}
        for t in range(8):
            r.append(lax.rsqrt(a[t, t]))
            for s in range(t + 1, 8):
                low[s, t] = a[s, t] * r[t]
            for u in range(t + 1, 8):
                for s in range(u, 8):
                    a[s, u] = a[s, u] - low[s, t] * low[u, t]
        z = []
        q = []
        for t in range(8):
            z_now, q_now = unit[t], rows[t]
            for s in range(t):
                z_now = z_now - low[t, s] * z[s]
                q_now = q_now - low[t, s] * q[s]
            z.append(z_now * r[t])
            q.append(q_now * r[t])
        y = [None] * 8
        for t in reversed(range(8)):
            y_now = z[t]
            for s in range(t + 1, 8):
                y_now = y_now - low[s, t] * y[s]
            y[t] = y_now * r[t]
        z_tile, q_tile, y_tile = z[0], q[0], y[0]
        for t in range(1, 8):
            z_tile = jnp.where(sub == t, z[t], z_tile)
            q_tile = jnp.where(sub == t, q[t], q_tile)
            y_tile = jnp.where(sub == t, y[t], y_tile)
        upper.append(jnp.where(lane >= o + sub, q_tile, F32(0)))
        tiles[p] = jnp.where(lane <= o + sub, z_tile, F32(0))
        for i in range(p + 1, min(p + 1 + NEAR, count)):
            terms = [by_lane(tiles[i], o + t) * y[t] for t in range(8)]
            while len(terms) > 1:
                terms = [terms[k] + terms[k + 1] for k in range(0, len(terms), 2)]
            tiles[i] = jnp.where(inside, F32(0), tiles[i]) - terms[0]
        far = p + 1 + NEAR
        if far < count:
            zero = jnp.zeros((8, BLK), F32)
            padded = jnp.concatenate([zero] * p + [y_tile] + [zero] * (count - p - 1), axis=0)
            less = exact_nn(jnp.concatenate(tiles[far:], axis=0), padded)
            for i in range(far, count):
                tiles[i] = jnp.where(inside, F32(0), tiles[i]) - less[8 * (i - far) : 8 * (i - far) + 8]
    return tiles, upper


def split(x):
    high = x.astype(BF16)
    return high, (x - high.astype(F32)).astype(BF16)


def dot_nt(a, b):
    return lax.dot_general(a, b, (((1,), (1,)), ((), ())), preferred_element_type=F32)


def dot_nn(a, b):
    return lax.dot_general(a, b, (((1,), (0,)), ((), ())), preferred_element_type=F32)


def pairs(dot, ah, al, bh, bl):
    return dot(ah, bh) + (dot(ah, bl) + dot(al, bh))


def exact_nt(a, b):
    return lax.dot_general(a, b, (((1,), (1,)), ((), ())), precision=lax.Precision.HIGHEST, preferred_element_type=F32)


def exact_nn(a, b):
    return jnp.dot(a, b, precision=lax.Precision.HIGHEST, preferred_element_type=F32)


def offset_of(index):
    return jnp.where(index == 3, 2, jnp.where(index == 2, 1, jnp.where(index == 1, -1, 0)))


EARLY = [
    (half, swapped, far, base)
    for half in range(2)
    for swapped in range(2)
    for far, base in ((0, 0), (-1, 0), (1, 0), (2, 0), (2, 2))
]
LATE = [(1, swapped, None, 0) for swapped in range(2)]


def load_leading(place, pieces, late, dest, sem, first_col):
    x, z, core = place[0], place[2], place[3]
    for ref, (half, swapped, far, base) in zip(pieces, LATE if late else EARLY, strict=True):

        def one(n, carry, ref=ref, base=base, far=far, half=half, swapped=swapped):
            i, y = n >> 1, n & 1
            if late:
                dx, dz = offset_of(i >> 2), offset_of(i & 3)
            else:
                near = offset_of(i + base)
                dx, dz = (near, far) if half == 1 else (far, near)
            block_row = ((x + dx) & 3) * 2 + y + 8 * half
            block_col = 8 * late + ((z + dz) & 3) * 2 + ((core + swapped) & 1) - first_col

            @pl.when((block_col >= 0) & (block_col < 4))
            def _():
                pltpu.make_async_copy(
                    ref.at[i, y],
                    dest.at[block_col, pl.ds(pl.multiple_of(block_row * BLK, BLK), BLK), :],
                    sem,
                ).start()

            return carry

        lax.fori_loop(0, ref.shape[0] * 2, one, 0)


def factor_kernel(call, place, *refs):
    late = call >= CALLS // 2
    count = len(LATE) if late else len(EARLY)
    pieces, refs = refs[:count], refs[count:]
    earlier = refs[: 2 * call]
    out_high, out_low, inv_high, inv_low = refs[2 * call : 4 + 2 * call]
    (lead, high, low, c, diag, inverse, upper, inverse1, low21, load_sem, strip_sem, out_sem) = refs[4 + 2 * call :]
    start = STRIP * call
    load_leading(place, pieces, late, lead, load_sem, 4 * call)
    copies = []
    for n in range(call):
        for which, dest in ((0, high), (1, low)):
            copies.append(
                pltpu.make_async_copy(
                    earlier[2 * n + which].at[pl.ds(start - STRIP * n, PW - start), :],
                    dest.at[:, pl.ds(STRIP * n, STRIP)],
                    strip_sem.at[2 * n + which],
                )
            )
    for copy in copies:
        copy.start()
    loaded = lead.at[:, PW // 2 :, :] if late else lead
    pltpu.make_async_copy(loaded, loaded, load_sem).wait()
    for copy in copies:
        copy.wait()

    def put(rows, cols, value):
        h, l = split(value)
        high[rows, cols] = h
        low[rows, cols] = l

    def before(kk):
        known = start + STEP * kk
        r0 = STEP * kk
        tiles = (PW - start - r0) // STEP

        def tile(t, carry):
            at = pl.multiple_of(r0 + t * STEP, STEP)
            rows = pl.ds(at, STEP)
            whole = pl.ds(pl.multiple_of(start + at, STEP), STEP)
            value = jnp.concatenate([lead[2 * kk, whole, :], lead[2 * kk + 1, whole, :]], axis=1)
            if known > 0:
                value = value - pairs(
                    dot_nt, high[rows, :known], low[rows, :known], high[r0 : r0 + STEP, :known], low[r0 : r0 + STEP, :known]
                )
            c[rows, :] = value
            return carry

        lax.fori_loop(0, tiles, tile, 0)
        diag[...] = c[r0 : r0 + BLK, :BLK]

    def between(kk):
        r0 = STEP * kk
        col = start + r0
        w1 = inverse[...]
        l21 = exact_nt(c[r0 + BLK : r0 + STEP, :BLK], w1)
        diag[...] = c[r0 + BLK : r0 + STEP, BLK:] - exact_nt(l21, l21)
        inverse1[...] = w1
        low21[...] = l21
        put(pl.ds(r0, BLK), pl.ds(col, BLK), upper[...].T)
        put(pl.ds(r0, BLK), pl.ds(col + BLK, BLK), jnp.zeros((BLK, BLK), F32))
        put(pl.ds(r0 + BLK, BLK), pl.ds(col, BLK), l21)

    def after(kk):
        r0 = STEP * kk
        col = start + r0
        w2 = inverse[...]
        put(pl.ds(r0 + BLK, BLK), pl.ds(col + BLK, BLK), upper[...].T)
        w21 = -exact_nn(w2, exact_nn(low21[...], inverse1[...]))
        top = jnp.concatenate([inverse1[...], jnp.zeros((BLK, BLK), F32)], axis=1)
        w = jnp.concatenate([top, jnp.concatenate([w21, w2], axis=1)], axis=0)
        wh, wl = split(w)
        inv_high[kk] = wh
        inv_low[kk] = wl
        tiles = (PW - start - r0) // STEP

        def tile(t, carry):
            rows = pl.ds(pl.multiple_of(r0 + t * STEP, STEP), STEP)
            ch, cl = split(c[rows, :])
            put(rows, pl.ds(col, STEP), pairs(dot_nt, ch, cl, inv_high[kk], inv_low[kk]))
            return carry

        lax.fori_loop(1, tiles, tile, 0)

    def half(h, carry):
        for kk in range(STRIP // STEP):
            pl.when(h == 2 * kk)(functools.partial(before, kk))
        w, u = eliminate([diag[8 * i : 8 * i + 8, :] for i in range(16)])
        for i in range(16):
            inverse[8 * i : 8 * i + 8, :] = w[i]
            upper[8 * i : 8 * i + 8, :] = u[i]
        for kk in range(STRIP // STEP):
            pl.when(h == 2 * kk)(functools.partial(between, kk))
            pl.when(h == 2 * kk + 1)(functools.partial(after, kk))
        return carry

    lax.fori_loop(0, STRIP // BLK, half, 0)
    outs = [
        pltpu.make_async_copy(high.at[:, pl.ds(start, STRIP)], out_high, out_sem.at[0]),
        pltpu.make_async_copy(low.at[:, pl.ds(start, STRIP)], out_low, out_sem.at[1]),
    ]
    for copy in outs:
        copy.start()
    for copy in outs:
        copy.wait()


def factor_strip(call, place, pieces, earlier):
    rows = PW - STRIP * call
    known = STRIP * (call + 1)
    strip = jax.ShapeDtypeStruct((rows, STRIP), BF16)
    inverses = jax.ShapeDtypeStruct((STRIP // STEP, STEP, STEP), BF16)
    block = pltpu.VMEM((BLK, BLK), F32)
    return pl.pallas_call(
        functools.partial(factor_kernel, call),
        out_shape=[strip, strip, inverses, inverses],
        in_specs=[SMEM] + [ANY] * (len(pieces) + 2 * call),
        out_specs=[ANY, ANY, VMEM, VMEM],
        scratch_shapes=[
            pltpu.VMEM((4, PW, BLK), F32),
            pltpu.VMEM((rows, known), BF16),
            pltpu.VMEM((rows, known), BF16),
            pltpu.VMEM((rows, STEP), F32),
            block,
            block,
            block,
            block,
            block,
            pltpu.SemaphoreType.DMA,
            pltpu.SemaphoreType.DMA((max(2 * call, 1),)),
            pltpu.SemaphoreType.DMA((2,)),
        ],
        compiler_params=PARAMS,
        cost_estimate=pl.CostEstimate(flops=int(4e10), bytes_accessed=int(1e8), transcendentals=0),
        name=f"factor{call}",
    )(place, *pieces, *earlier)


def assemble_kernel(source, valid, colsel, front, f0, f1, g0, g1, out):
    q = pl.program_id(0)
    del source
    out[:, :BLK] = front[:, :BLK]
    for n in range(5):
        cols = slice(n * BLK, (n + 1) * BLK)
        total = front[:, cols]
        for child, (first, rest) in enumerate(((f0, g0), (f1, g1))):
            use = valid[child, q]
            sel = colsel[child, n]

            def block(j, first=first, rest=rest):
                return first[0, 0] if j == 0 else rest[0, 0, :, (j - 1) * BLK : j * BLK]

            if n < 4:
                total = total + jnp.where((sel == 1) & (use == 1), block(n), F32(0))
            if n > 0:
                total = total + jnp.where((sel == 2) & (use == 1), block(n - 1), F32(0))
        out[:, cols] = total


def assemble(source, valid, colsel, front, first, rest):
    def pick(child):
        return lambda q, s, v, c: (q % 2, s[child, q], 0, 0)

    rows, cols = front.shape
    return pl.pallas_call(
        assemble_kernel,
        out_shape=jax.ShapeDtypeStruct(front.shape, F32),
        grid_spec=pltpu.PrefetchScalarGridSpec(
            num_scalar_prefetch=3,
            grid=(rows // BLK,),
            in_specs=[
                pl.BlockSpec((BLK, cols), lambda q, *_: (q, 0)),
                pl.BlockSpec((1, 1, BLK, BLK), pick(0)),
                pl.BlockSpec((1, 1, BLK, BLK), pick(1)),
                pl.BlockSpec((1, 1, BLK, 3 * BLK), pick(0)),
                pl.BlockSpec((1, 1, BLK, 3 * BLK), pick(1)),
            ],
            out_specs=pl.BlockSpec((BLK, cols), lambda q, *_: (q, 0)),
        ),
        compiler_params=PARAMS,
        name="assemble",
    )(source, valid, colsel, front, first, first, rest, rest)


def solve_kernel(place, *refs):
    strips, inverses, slabs = refs[:8], refs[8:16], refs[16:24]
    panel_rows, asm, panel_out, trailing = refs[24:28]
    high, low, xh, xl, yh, yl, raw, yraw, sems, raw_sem, slab_sem = refs[28:]
    x, y, z, core = place[0], place[1], place[2], place[3]
    row = x * 2 + y % 2
    col = (y // 2) * 8 + z * 2 + core
    wait_strip = []
    for n in range(CALLS):
        for which, dest in ((0, high), (1, low)):
            copy = pltpu.make_async_copy(
                strips[2 * n + which],
                dest.at[pl.ds(STRIP * n, PW - STRIP * n), pl.ds(STRIP * n, STRIP)],
                sems.at[2 * n + which],
            )
            wait_strip.append(copy)
    raws = [pltpu.make_async_copy(panel_rows.at[pl.ds(4 * n, 4)], raw.at[pl.ds(4 * n, 4)], raw_sem.at[n]) for n in range(4)]
    slab_copies = []
    for dx in range(4):
        for dl in range(2):
            there = ((x + dx) % 4) * 2 + (y + dl) % 2
            for second in range(2):
                at = pl.multiple_of((there + 8 * second) * BLK, BLK)
                slab_copies.append(
                    pltpu.make_async_copy(
                        slabs[dx * 2 + dl].at[pl.ds(second * BLK, BLK), :],
                        yraw.at[pl.ds(at, BLK), :],
                        slab_sem.at[(dx * 2 + dl) * 2 + second],
                    )
                )
    raws[0].start()
    for copy in slab_copies:
        copy.start()
    for n in range(CALLS):
        wait_strip[2 * n].start()
        wait_strip[2 * n + 1].start()
        if n:
            raws[n].start()
    for copy in slab_copies:
        copy.wait()
    panel_out[: 2 * BLK, :] = jnp.zeros((2 * BLK, BLK), F32)
    for k in range(PW // STEP):
        known = STEP * k
        if k % 2 == 0:
            raws[k // 2].wait()
            wait_strip[k].wait()
            wait_strip[k + 1].wait()
        wh, wl = inverses[2 * (k // 2)], inverses[2 * (k // 2) + 1]
        here = slice(known, known + STEP)
        value = yraw[here, :]
        if k:
            value = value - pairs(dot_nn, high[here, :known], low[here, :known], yh[:known, :], yl[:known, :])
        vh, vl = split(value)
        got = pairs(dot_nn, wh[k % 2], wl[k % 2], vh, vl)
        yh[here, :], yl[here, :] = split(got)

        def tile(t, carry, k=k, known=known, here=here, wh=wh, wl=wl):
            rows = pl.ds(pl.multiple_of(t * 512, 512), 512)
            value = jnp.concatenate([raw[2 * k, rows, :], raw[2 * k + 1, rows, :]], axis=1)
            if k:
                value = value - pairs(dot_nt, xh[rows, :known], xl[rows, :known], high[here, :known], low[here, :known])
            vh, vl = split(value)
            got = pairs(dot_nt, vh, vl, wh[k % 2], wl[k % 2])
            xh[rows, here], xl[rows, here] = split(got)
            for side in range(2):

                @pl.when(col == 2 * k + side)
                def _():
                    panel_out[pl.ds(pl.multiple_of(2 * BLK + t * 512, BLK), 512), :] = got[:, side * BLK : (side + 1) * BLK]

            return carry

        lax.fori_loop(0, raw.shape[1] // 512, tile, 0)
    lanes = pl.ds(pl.multiple_of(col * BLK, BLK), BLK)
    for second in range(2):
        block_row = row + 8 * second

        @pl.when(block_row >= col)
        def _():
            rows = pl.ds(pl.multiple_of(block_row * BLK, BLK), BLK)
            panel_out[second * BLK : (second + 1) * BLK, :] = high[rows, lanes].astype(F32) + low[rows, lanes].astype(F32)

    trailing[: 2 * BLK, :] = jnp.zeros((2 * BLK, trailing.shape[1]), F32)
    trailing[:, :BLK] = jnp.zeros((trailing.shape[0], BLK), F32)

    def update(t, carry):
        rows = pl.ds(pl.multiple_of(t * 512, 512), 512)
        out = pl.ds(pl.multiple_of(2 * BLK + t * 512, STEP), 512)
        trailing[out, BLK:] = asm[out, BLK:] - pairs(dot_nn, xh[rows, :], xl[rows, :], yh[...], yl[...])
        return carry

    lax.fori_loop(0, raw.shape[1] // 512, update, 0)


def solve(place, strips, inverses, slabs, panel_rows, asm):
    rows, cols = asm.shape
    under = rows - 2 * BLK
    return pl.pallas_call(
        solve_kernel,
        out_shape=[jax.ShapeDtypeStruct((rows, BLK), F32), jax.ShapeDtypeStruct((rows, cols), F32)],
        in_specs=[SMEM] + [ANY] * 8 + [VMEM] * 8 + [ANY] * 9 + [VMEM],
        out_specs=[VMEM, VMEM],
        scratch_shapes=[
            pltpu.VMEM((PW, PW), BF16),
            pltpu.VMEM((PW, PW), BF16),
            pltpu.VMEM((under, PW), BF16),
            pltpu.VMEM((under, PW), BF16),
            pltpu.VMEM((PW, cols - BLK), BF16),
            pltpu.VMEM((PW, cols - BLK), BF16),
            pltpu.VMEM((16, under, BLK), F32),
            pltpu.VMEM((PW, cols - BLK), F32),
            pltpu.SemaphoreType.DMA((8,)),
            pltpu.SemaphoreType.DMA((4,)),
            pltpu.SemaphoreType.DMA((16,)),
        ],
        compiler_params=PARAMS,
        name="solve",
    )(place, *strips, *inverses, *slabs, panel_rows, asm)


def local(front, updates, maps):
    row_at = lax.axis_index("row")
    col_at = lax.axis_index("col")
    place = jnp.stack([row_at // 2, (col_at // 8) * 2 + row_at % 2, (col_at // 2) % 4, col_at % 2]).astype(jnp.int32)
    slots = maps >> 4
    row_slots = lax.dynamic_index_in_dim(slots.reshape(2, 2, 8, 4), row_at, 2, keepdims=False)
    col_slots = lax.dynamic_index_in_dim(slots.reshape(2, 16, 4), col_at, 1, keepdims=False)

    first = lax.all_to_all(updates[:, :BLK].reshape(2, 8, BLK, BLK), "row", split_axis=1, concat_axis=1, tiled=True)
    meets = col_slots[:, 0] == 0
    panel = front[:, :BLK].reshape(5, 2, BLK, BLK)
    parts = []
    for m in range(5):
        total = panel[m]
        for child in range(2):
            for a in (m, m - 1):
                if 0 <= a < 4:
                    hit = (row_slots[child, :, a] == m) & meets[child]
                    total = total + jnp.where(hit[:, None, None], first[:, 4 * child + a], F32(0))
        parts.append(total)
    corner = parts[0].reshape(2 * BLK, BLK)
    under = jnp.stack(parts[1:]).reshape(8 * BLK, BLK)
    pieces, late = gather_leading(corner, place[1])

    tokens = [pieces[8][0, 0, 0, 0], pieces[9][0, 0, 0, 0], pieces[18][0, 0, 0, 0], pieces[19][0, 0, 0, 0]]
    panel_rows = lax.all_gather(settled(under, *tokens), "col", axis=0, tiled=True).reshape(16, 8 * BLK, BLK)
    late = along_x(settled(late, *tokens))
    late_pieces = []

    strips, inverses = [], []

    def factor(call, place):
        got = factor_strip(call, place, late_pieces if call >= CALLS // 2 else pieces, strips)
        strips.extend(got[:2])
        inverses.extend(got[2:])
        return got[2][0, 0, 0].astype(F32)

    token = factor(0, place)
    late = settled(jnp.concatenate(late), token)
    late_pieces += [late, move(late, dcore=1)]
    others = settled(updates[:, BLK:], token)
    rest = lax.all_to_all(others.reshape(2, 8, BLK, 3 * BLK), "row", split_axis=1, concat_axis=1, tiled=True)
    token = factor(1, place)

    slot = jnp.arange(5)
    own = jnp.pad(row_slots, ((0, 0), (0, 0), (0, 1)), constant_values=-1) == slot
    prior = jnp.pad(row_slots, ((0, 0), (0, 0), (1, 0)), constant_values=-1) == slot
    valid = (own | prior).astype(jnp.int32)
    source = jnp.where(own, slot, jnp.where(prior, slot - 1, 0)) + 4 * jnp.arange(2)[:, None, None]
    valid = valid.transpose(0, 2, 1).reshape(2, 10)
    source = source.transpose(0, 2, 1).reshape(2, 10).astype(jnp.int32)
    own = jnp.pad(col_slots, ((0, 0), (0, 1)), constant_values=-1) == slot
    prior = jnp.pad(col_slots, ((0, 0), (1, 0)), constant_values=-1) == slot
    colsel = jnp.where(own, 1, jnp.where(prior, 2, 0)).astype(jnp.int32)
    asm = assemble(source, settled(valid, token), colsel, front, first, rest)
    head = asm[: 2 * BLK, BLK:]
    slabs = []
    for dx in range(4):
        for dl in range(2):
            if dx == 0 and dl == 0:
                slabs.append(head)
                continue
            there = [(r, ((r // 2 - dx) % 4) * 2 + (r + dl) % 2) for r in range(8)]
            slabs.append(lax.ppermute(head, "row", there))
    factor(2, settled(place, asm[0, 0]))
    factor(3, place)
    return tuple(solve(place, strips, inverses, slabs, panel_rows, asm))


def solution(mesh):
    in_specs = (P("row", "col"), P("row", "col"), P())
    out_specs = (P("row", "col"), P("row", "col"))
    return jax.shard_map(local, mesh=mesh, in_specs=in_specs, out_specs=out_specs, check_vma=False)
```

```python
import functools

import jax
import jax.numpy as jnp
from jax import lax
from jax.experimental import pallas as pl
from jax.experimental.pallas import tpu as pltpu
from jax.sharding import PartitionSpec as P

BLK = 128
PW = 2048
STRIPS = ((0, 1024), (1024, 512), (1536, 512))
STEP = 256
BOTH = ("row", "col")
OFFSETS = (0, -1, 1, 2)
NEAR = 2
F32 = jnp.float32
BF16 = jnp.bfloat16
PARAMS = pltpu.CompilerParams(vmem_limit_bytes=58 << 20)
ANY = pl.BlockSpec(memory_space=pl.ANY)
VMEM = pl.BlockSpec(memory_space=pltpu.VMEM)
SMEM = pl.BlockSpec(memory_space=pltpu.SMEM)


def flat(x, y, z, core):
    return ((x % 4) * 2 + y % 2) * 16 + ((y % 4) // 2) * 8 + (z % 4) * 2 + core % 2


def move(value, *by):
    every = [(x, y, z, c) for x in range(4) for y in range(4) for z in range(4) for c in range(2)]
    pairs = []
    for x, y, z, c in every:
        step = by[c] if len(by) > 1 else by[0]
        if step is not None:
            pairs.append((flat(x, y, z, c), flat(x + step[0], y + step[1], z + step[2], c + step[3])))
    return lax.ppermute(value, BOTH, pairs)


SWAP = (0, 0, 0, 1)


def around(value, *axes):
    out = [value]
    for offset in OFFSETS[1:]:
        out.append(move(value, *[tuple(-offset if n == axis else 0 for n in range(4)) for axis in axes]))
    return out


def settled(value, *tokens):
    ready = functools.reduce(jnp.logical_and, [token <= F32(jnp.finfo(jnp.float32).max) for token in tokens])
    return jnp.where(ready, value, jnp.zeros((), value.dtype))


def gather_leading(corner, y_at, core_at):
    first = core_at == 0
    upper, lower = corner[:BLK], corner[BLK:]
    mine = jnp.where(first, upper, lower)
    other = move(jnp.where(first, lower, upper), SWAP)
    both = jnp.stack([jnp.where(first, mine, other), jnp.where(first, other, mine)])
    own, below, above, opposite = around(both, 1)
    blocks = []
    for y in range(4):
        d = (y - y_at) & 3
        blocks.append(jnp.where(d == 0, own, jnp.where(d == 1, above, jnp.where(d == 2, opposite, below))))
    group = jnp.stack(around(jnp.stack(blocks), 2, 0))
    mine = around(group[:, :2], 0, 2)
    pieces = [*mine, *[move(piece, SWAP) for piece in mine]]
    late = jnp.where(first, move(group[:, 2], SWAP), group[:, 3])
    return pieces, late


def eliminate(tiles):
    tiles = list(tiles)
    count = len(tiles)
    lane = lax.broadcasted_iota(jnp.int32, (8, BLK), 1)
    sub = lax.broadcasted_iota(jnp.int32, (8, BLK), 0)
    upper = []

    def by_lane(x, j):
        return jnp.broadcast_to(x[:, j : j + 1], (8, BLK))

    def by_sub(x, s):
        return jnp.broadcast_to(x[s : s + 1, :], (8, BLK))

    for p in range(count):
        now = tiles[p]
        o = 8 * p
        inside = (lane >= o) & (lane < o + 8)
        column = [by_lane(now, o + t) for t in range(8)]
        a = {(s, t): by_sub(column[t], s) for t in range(8) for s in range(t, 8)}
        rows = [by_sub(now, t) for t in range(8)]
        unit = [jnp.where(lane == o + t, F32(1), jnp.where(inside, F32(0), rows[t])) for t in range(8)]
        r = []
        low = {}
        for t in range(8):
            r.append(lax.rsqrt(a[t, t]))
            for s in range(t + 1, 8):
                low[s, t] = a[s, t] * r[t]
            for u in range(t + 1, 8):
                for s in range(u, 8):
                    a[s, u] = a[s, u] - low[s, t] * low[u, t]
        z = []
        q = []
        for t in range(8):
            z_now, q_now = unit[t], rows[t]
            for s in range(t):
                z_now = z_now - low[t, s] * z[s]
                q_now = q_now - low[t, s] * q[s]
            z.append(z_now * r[t])
            q.append(q_now * r[t])
        y = [None] * 8
        for t in reversed(range(8)):
            y_now = z[t]
            for s in range(t + 1, 8):
                y_now = y_now - low[s, t] * y[s]
            y[t] = y_now * r[t]
        z_tile, q_tile, y_tile = z[0], q[0], y[0]
        for t in range(1, 8):
            z_tile = jnp.where(sub == t, z[t], z_tile)
            q_tile = jnp.where(sub == t, q[t], q_tile)
            y_tile = jnp.where(sub == t, y[t], y_tile)
        upper.append(jnp.where(lane >= o + sub, q_tile, F32(0)))
        tiles[p] = jnp.where(lane <= o + sub, z_tile, F32(0))
        for i in range(p + 1, min(p + 1 + NEAR, count)):
            terms = [by_lane(tiles[i], o + t) * y[t] for t in range(8)]
            while len(terms) > 1:
                terms = [terms[k] + terms[k + 1] for k in range(0, len(terms), 2)]
            tiles[i] = jnp.where(inside, F32(0), tiles[i]) - terms[0]
        far = p + 1 + NEAR
        if far < count:
            zero = jnp.zeros((8, BLK), F32)
            padded = jnp.concatenate([zero] * p + [y_tile] + [zero] * (count - p - 1), axis=0)
            less = exact_nn(jnp.concatenate(tiles[far:], axis=0), padded)
            for i in range(far, count):
                tiles[i] = jnp.where(inside, F32(0), tiles[i]) - less[8 * (i - far) : 8 * (i - far) + 8]
    return tiles, upper


def split(x):
    high = x.astype(BF16)
    return high, (x - high.astype(F32)).astype(BF16)


def dot_nt(a, b):
    return lax.dot_general(a, b, (((1,), (1,)), ((), ())), preferred_element_type=F32)


def dot_nn(a, b):
    return lax.dot_general(a, b, (((1,), (0,)), ((), ())), preferred_element_type=F32)


def pairs(dot, ah, al, bh, bl):
    return dot(ah, bh) + (dot(ah, bl) + dot(al, bh))


def exact_nt(a, b):
    return lax.dot_general(a, b, (((1,), (1,)), ((), ())), precision=lax.Precision.HIGHEST, preferred_element_type=F32)


def exact_nn(a, b):
    return jnp.dot(a, b, precision=lax.Precision.HIGHEST, preferred_element_type=F32)


def offset_of(index):
    return jnp.where(index == 3, 2, jnp.where(index == 2, 1, jnp.where(index == 1, -1, 0)))


def load_leading(place, pieces, late, dest, sems, first_col):
    x, z, core = place[0], place[2], place[3]
    count = dest.shape[0]

    def fetch(source, block_row, block_col):
        pltpu.make_async_copy(
            source,
            dest.at[block_col, pl.ds(pl.multiple_of(block_row * BLK, BLK), BLK), :],
            sems.at[block_col >> 2],
        ).start()

    if late:
        for swapped, ref in enumerate(pieces):
            low_y = (core + swapped) & 1

            def one(n, carry, ref=ref, low_y=low_y):
                far, near, c = n >> 3, (n >> 1) & 3, n & 1
                block_row = ((x + offset_of(near)) & 3) * 2 + low_y + 8
                block_col = 8 + ((z + offset_of(far)) & 3) * 2 + c - first_col

                @pl.when((block_col >= 0) & (block_col < count))
                def _():
                    fetch(ref.at[far, near, c], block_row, block_col)

                return carry

            lax.fori_loop(0, 32, one, 0)
        return
    for number, ref in enumerate(pieces):
        half = (core + number // 4) & 1
        far = OFFSETS[number % 4]

        def one(n, carry, ref=ref, half=half, far=far):
            i, y, c = n >> 2, (n >> 1) & 1, n & 1
            near = offset_of(i)
            dx, dz = jnp.where(half == 0, far, near), jnp.where(half == 0, near, far)
            fetch(ref.at[i, y, c], ((x + dx) & 3) * 2 + y + 8 * half, ((z + dz) & 3) * 2 + c - first_col)
            return carry

        lax.fori_loop(0, 16, one, 0)


def factor_kernel(call, place, *refs):
    start, width = STRIPS[call]
    late = start >= PW // 2
    count = 2 if late else 8
    pieces, refs = refs[:count], refs[count:]
    earlier = refs[: 2 * call]
    out_high, out_low, inv_high, inv_low = refs[2 * call : 4 + 2 * call]
    (lead, high, low, c, diag, inverse, upper, inverse1, low21, load_sem, strip_sem, out_sem) = refs[4 + 2 * call :]
    load_leading(place, pieces, late, lead, load_sem, start // BLK)
    copies = []
    for n in range(call):
        for which, dest in ((0, high), (1, low)):
            copies.append(
                pltpu.make_async_copy(
                    earlier[2 * n + which].at[pl.ds(start - STRIPS[n][0], PW - start), :],
                    dest.at[:, pl.ds(*STRIPS[n])],
                    strip_sem.at[2 * n + which],
                )
            )
    for copy in copies:
        copy.start()

    def wait_lead(n):
        loaded = lead.at[4 * n : 4 * n + 4, PW // 2 if late else 0 :, :]
        pltpu.make_async_copy(loaded, loaded, load_sem.at[n]).wait()

    def outs(kk):
        rows, cols = pl.ds(STEP * kk, PW - start - STEP * kk), pl.ds(STEP * kk, STEP)
        source = pl.ds(start + STEP * kk, STEP)
        return [
            pltpu.make_async_copy(high.at[rows, source], out_high.at[rows, cols], out_sem.at[2 * kk]),
            pltpu.make_async_copy(low.at[rows, source], out_low.at[rows, cols], out_sem.at[2 * kk + 1]),
        ]

    wait_lead(0)
    for copy in copies:
        copy.wait()

    def put(rows, cols, value):
        h, l = split(value)
        high[rows, cols] = h
        low[rows, cols] = l

    def before(kk):
        if kk and kk % 2 == 0:
            wait_lead(kk // 2)
        known = start + STEP * kk
        r0 = STEP * kk
        tiles = (PW - start - r0) // STEP

        def tile(t, carry):
            at = pl.multiple_of(r0 + t * STEP, STEP)
            rows = pl.ds(at, STEP)
            whole = pl.ds(pl.multiple_of(start + at, STEP), STEP)
            value = jnp.concatenate([lead[2 * kk, whole, :], lead[2 * kk + 1, whole, :]], axis=1)
            if known > 0:
                value = value - pairs(
                    dot_nt, high[rows, :known], low[rows, :known], high[r0 : r0 + STEP, :known], low[r0 : r0 + STEP, :known]
                )
            c[rows, :] = value
            return carry

        lax.fori_loop(0, tiles, tile, 0)
        diag[...] = c[r0 : r0 + BLK, :BLK]

    def between(kk):
        r0 = STEP * kk
        col = start + r0
        w1 = inverse[...]
        l21 = exact_nt(c[r0 + BLK : r0 + STEP, :BLK], w1)
        diag[...] = c[r0 + BLK : r0 + STEP, BLK:] - exact_nt(l21, l21)
        inverse1[...] = w1
        low21[...] = l21
        put(pl.ds(r0, BLK), pl.ds(col, BLK), upper[...].T)
        put(pl.ds(r0, BLK), pl.ds(col + BLK, BLK), jnp.zeros((BLK, BLK), F32))
        put(pl.ds(r0 + BLK, BLK), pl.ds(col, BLK), l21)

    def after(kk):
        r0 = STEP * kk
        col = start + r0
        w2 = inverse[...]
        put(pl.ds(r0 + BLK, BLK), pl.ds(col + BLK, BLK), upper[...].T)
        w21 = -exact_nn(w2, exact_nn(low21[...], inverse1[...]))
        top = jnp.concatenate([inverse1[...], jnp.zeros((BLK, BLK), F32)], axis=1)
        w = jnp.concatenate([top, jnp.concatenate([w21, w2], axis=1)], axis=0)
        wh, wl = split(w)
        inv_high[kk] = wh
        inv_low[kk] = wl
        tiles = (PW - start - r0) // STEP

        def tile(t, carry):
            rows = pl.ds(pl.multiple_of(r0 + t * STEP, STEP), STEP)
            ch, cl = split(c[rows, :])
            put(rows, pl.ds(col, STEP), pairs(dot_nt, ch, cl, inv_high[kk], inv_low[kk]))
            return carry

        lax.fori_loop(1, tiles, tile, 0)
        for copy in outs(kk):
            copy.start()

    def half(h, carry):
        for kk in range(width // STEP):
            pl.when(h == 2 * kk)(functools.partial(before, kk))
        w, u = eliminate([diag[8 * i : 8 * i + 8, :] for i in range(16)])
        for i in range(16):
            inverse[8 * i : 8 * i + 8, :] = w[i]
            upper[8 * i : 8 * i + 8, :] = u[i]
        for kk in range(width // STEP):
            pl.when(h == 2 * kk)(functools.partial(between, kk))
            pl.when(h == 2 * kk + 1)(functools.partial(after, kk))
        return carry

    lax.fori_loop(0, width // BLK, half, 0)
    for kk in range(width // STEP):
        for copy in outs(kk):
            copy.wait()


def factor_strip(call, place, pieces, earlier):
    start, width = STRIPS[call]
    rows = PW - start
    known = start + width
    strip = jax.ShapeDtypeStruct((rows, width), BF16)
    inverses = jax.ShapeDtypeStruct((width // STEP, STEP, STEP), BF16)
    block = pltpu.VMEM((BLK, BLK), F32)
    return pl.pallas_call(
        functools.partial(factor_kernel, call),
        out_shape=[strip, strip, inverses, inverses],
        in_specs=[SMEM] + [ANY] * (len(pieces) + 2 * call),
        out_specs=[ANY, ANY, VMEM, VMEM],
        scratch_shapes=[
            pltpu.VMEM((width // BLK, PW, BLK), F32),
            pltpu.VMEM((rows, known), BF16),
            pltpu.VMEM((rows, known), BF16),
            pltpu.VMEM((rows, STEP), F32),
            block,
            block,
            block,
            block,
            block,
            pltpu.SemaphoreType.DMA((width // 512,)),
            pltpu.SemaphoreType.DMA((max(2 * call, 1),)),
            pltpu.SemaphoreType.DMA((2 * width // STEP,)),
        ],
        compiler_params=PARAMS,
        cost_estimate=pl.CostEstimate(flops=int(7e7) * width, bytes_accessed=int(1e8), transcendentals=0),
        name=f"factor{call}",
    )(place, *pieces, *earlier)


def solve_kernel(place, source, colsel, *refs):
    n_strips = 2 * len(STRIPS)
    strips, inverses, refs = refs[:n_strips], refs[n_strips : 2 * n_strips], refs[2 * n_strips :]
    slabs, refs = refs[:8], refs[8:]
    panel_rows, front, first, rest, panel_out, trailing = refs[:6]
    high, low, xh, xl, yh, yl, raw, yraw, base, child, sems, raw_sem, slab_sem, child_sem = refs[6:]
    x, y, z, core = place[0], place[1], place[2], place[3]
    row = x * 2 + y % 2
    col = (y // 2) * 8 + z * 2 + core
    wait_strip = {}
    for n, (start, width) in enumerate(STRIPS):
        rows, cols = pl.ds(start, PW - start), pl.ds(start, width)
        wait_strip[start] = [
            pltpu.make_async_copy(strips[2 * n + which], dest.at[rows, cols], sems.at[2 * n + which])
            for which, dest in ((0, high), (1, low))
        ]
    raws = [pltpu.make_async_copy(panel_rows.at[pl.ds(4 * n, 4)], raw.at[pl.ds(4 * n, 4)], raw_sem.at[n]) for n in range(4)]
    slab_copies = []
    for dx in range(4):
        for dl in range(2):
            there = ((x + dx) % 4) * 2 + (y + dl) % 2
            for second in range(2):
                at = pl.multiple_of((there + 8 * second) * BLK, BLK)
                slab_copies.append(
                    pltpu.make_async_copy(
                        slabs[dx * 2 + dl].at[pl.ds(second * BLK, BLK), :],
                        yraw.at[pl.ds(at, BLK), :],
                        slab_sem.at[(dx * 2 + dl) * 2 + second],
                    )
                )
    raws[0].start()
    for copy in slab_copies:
        copy.start()
    for copies in wait_strip.values():
        for copy in copies:
            copy.start()
    for copy in raws[1:]:
        copy.start()
    children = [
        pltpu.make_async_copy(front.at[2 * BLK :, BLK:], base, child_sem.at[0]),
        pltpu.make_async_copy(first, child.at[:, :, :, pl.ds(0, BLK)], child_sem.at[1]),
        pltpu.make_async_copy(rest, child.at[:, :, :, pl.ds(BLK, 3 * BLK)], child_sem.at[2]),
    ]
    for copy in children:
        copy.start()
    for copy in slab_copies:
        copy.wait()
    panel_out[: 2 * BLK, :] = jnp.zeros((2 * BLK, BLK), F32)
    for k in range(PW // STEP):
        known = STEP * k
        if k % 2 == 0:
            raws[k // 2].wait()
        for copy in wait_strip.get(known, ()):
            copy.wait()
        strip = max(n for n, (start, _) in enumerate(STRIPS) if start <= known)
        wh, wl = inverses[2 * strip], inverses[2 * strip + 1]
        inner = k - STRIPS[strip][0] // STEP
        here = slice(known, known + STEP)
        value = yraw[here, :]
        if k:
            value = value - pairs(dot_nn, high[here, :known], low[here, :known], yh[:known, :], yl[:known, :])
        vh, vl = split(value)
        got = pairs(dot_nn, wh[inner], wl[inner], vh, vl)
        yh[here, :], yl[here, :] = split(got)

        def tile(t, carry, k=k, known=known, here=here, wh=wh, wl=wl, inner=inner):
            rows = pl.ds(pl.multiple_of(t * 512, 512), 512)
            value = jnp.concatenate([raw[2 * k, rows, :], raw[2 * k + 1, rows, :]], axis=1)
            if k:
                value = value - pairs(dot_nt, xh[rows, :known], xl[rows, :known], high[here, :known], low[here, :known])
            vh, vl = split(value)
            got = pairs(dot_nt, vh, vl, wh[inner], wl[inner])
            xh[rows, here], xl[rows, here] = split(got)
            for side in range(2):

                @pl.when(col == 2 * k + side)
                def _():
                    panel_out[pl.ds(pl.multiple_of(2 * BLK + t * 512, BLK), 512), :] = got[:, side * BLK : (side + 1) * BLK]

            return carry

        lax.fori_loop(0, raw.shape[1] // 512, tile, 0)
    lanes = pl.ds(pl.multiple_of(col * BLK, BLK), BLK)
    for second in range(2):
        block_row = row + 8 * second

        @pl.when(block_row >= col)
        def _():
            rows = pl.ds(pl.multiple_of(block_row * BLK, BLK), BLK)
            panel_out[second * BLK : (second + 1) * BLK, :] = high[rows, lanes].astype(F32) + low[rows, lanes].astype(F32)

    trailing[: 2 * BLK, :] = jnp.zeros((2 * BLK, trailing.shape[1]), F32)
    trailing[:, :BLK] = jnp.zeros((trailing.shape[0], BLK), F32)

    for copy in children:
        copy.wait()

    def assemble(q, carry):
        rows = pl.ds(pl.multiple_of(q * BLK, BLK), BLK)
        out = pl.ds(pl.multiple_of((q + 2) * BLK, BLK), BLK)
        for n in range(1, 5):
            total = base[rows, (n - 1) * BLK : n * BLK]
            for k in range(2):
                at = source[k, q + 2]
                use = at >= 0
                at = jnp.maximum(at, 0)
                for sel, j in ((1, n), (2, n - 1)):
                    if j < 4:
                        block = child[at, q & 1, :, j * BLK : (j + 1) * BLK]
                        total = total + jnp.where(use & (colsel[k, n] == sel), block, F32(0))
            trailing[out, n * BLK : (n + 1) * BLK] = total
        return carry

    lax.fori_loop(0, 8, assemble, 0)

    def update(t, carry):
        rows = pl.ds(pl.multiple_of(t * 512, 512), 512)
        out = pl.ds(pl.multiple_of(2 * BLK + t * 512, STEP), 512)
        trailing[out, BLK:] = trailing[out, BLK:] - pairs(dot_nn, xh[rows, :], xl[rows, :], yh[...], yl[...])
        return carry

    lax.fori_loop(0, raw.shape[1] // 512, update, 0)


def solve(place, source, colsel, strips, inverses, slabs, panel_rows, front, first, rest):
    rows, cols = front.shape
    under = rows - 2 * BLK
    return pl.pallas_call(
        solve_kernel,
        out_shape=[jax.ShapeDtypeStruct((rows, BLK), F32), jax.ShapeDtypeStruct((rows, cols), F32)],
        in_specs=[SMEM] * 3 + [ANY] * len(strips) + [VMEM] * len(inverses) + [ANY] * 12,
        out_specs=[VMEM, VMEM],
        scratch_shapes=[
            pltpu.VMEM((PW, PW), BF16),
            pltpu.VMEM((PW, PW), BF16),
            pltpu.VMEM((under, PW), BF16),
            pltpu.VMEM((under, PW), BF16),
            pltpu.VMEM((PW, cols - BLK), BF16),
            pltpu.VMEM((PW, cols - BLK), BF16),
            pltpu.VMEM((16, under, BLK), F32),
            pltpu.VMEM((PW, cols - BLK), F32),
            pltpu.VMEM((under, cols - BLK), F32),
            pltpu.VMEM((8, 2, BLK, 4 * BLK), F32),
            pltpu.SemaphoreType.DMA((len(strips),)),
            pltpu.SemaphoreType.DMA((4,)),
            pltpu.SemaphoreType.DMA((16,)),
            pltpu.SemaphoreType.DMA((3,)),
        ],
        compiler_params=PARAMS,
        name="solve",
    )(place, source, colsel, *strips, *inverses, *slabs, panel_rows, front, first, rest)


def local(front, updates, maps):
    row_at = lax.axis_index("row")
    col_at = lax.axis_index("col")
    place = jnp.stack([row_at // 2, (col_at // 8) * 2 + row_at % 2, (col_at // 2) % 4, col_at % 2]).astype(jnp.int32)
    slots = maps >> 4
    row_slots = lax.dynamic_index_in_dim(slots.reshape(2, 2, 8, 4), row_at, 2, keepdims=False)
    col_slots = lax.dynamic_index_in_dim(slots.reshape(2, 16, 4), col_at, 1, keepdims=False)

    slot = jnp.arange(5)
    own = jnp.pad(row_slots, ((0, 0), (0, 0), (0, 1)), constant_values=-1) == slot
    prior = jnp.pad(row_slots, ((0, 0), (0, 0), (1, 0)), constant_values=-1) == slot
    source = jnp.where(own, slot, jnp.where(prior, slot - 1, -8)) + 4 * jnp.arange(2)[:, None, None]
    source = source.transpose(0, 2, 1).reshape(2, 10).astype(jnp.int32)
    own = jnp.pad(col_slots, ((0, 0), (0, 1)), constant_values=-1) == slot
    prior = jnp.pad(col_slots, ((0, 0), (1, 0)), constant_values=-1) == slot
    colsel = jnp.where(own, 1, jnp.where(prior, 2, 0)).astype(jnp.int32)

    def exchange(part):
        outgoing = part.reshape(2, 8, BLK, part.shape[1]).transpose(1, 0, 2, 3)
        return lax.all_to_all(outgoing, "row", split_axis=0, concat_axis=0, tiled=True)

    first = exchange(updates[:, :BLK])
    meets = col_slots[:, 0] == 0
    panel = front[:, :BLK].reshape(5, 2, BLK, BLK)
    parts = []
    for m in range(5):
        total = panel[m]
        for child in range(2):
            for a in (m, m - 1):
                if 0 <= a < 4:
                    hit = (row_slots[child, :, a] == m) & meets[child]
                    total = total + jnp.where(hit[:, None, None], first[4 * child + a], F32(0))
        parts.append(total)
    corner = parts[0].reshape(2 * BLK, BLK)
    under = jnp.stack(parts[1:]).reshape(8 * BLK, BLK)
    pieces, late = gather_leading(corner, place[1], place[3])

    tokens = [piece[0, 0, 0, 0, 0] for piece in pieces[5:]]
    panel_rows = lax.all_gather(settled(under, *tokens), "col", axis=0, tiled=True).reshape(16, 8 * BLK, BLK)
    late = around(settled(late, *tokens), 2)
    rest = exchange(settled(updates[:, BLK:], *tokens))

    strips, inverses = [], []

    def factor(call, place, pieces):
        got = factor_strip(call, place, pieces, strips)
        strips.extend(got[:2])
        inverses.extend(got[2:])
        return got[2][0, 0, 0].astype(F32)

    token = factor(0, place, pieces)
    late = settled(jnp.stack(late), token)
    late = [late, move(late, SWAP)]
    head = front[: 2 * BLK, BLK:].reshape(2, BLK, 4, BLK)
    for child in range(2):
        blocks = jnp.concatenate([first[4 * child], rest[4 * child]], axis=2).reshape(2, BLK, 4, BLK)
        ahead = jnp.concatenate([blocks[:, :, 1:], jnp.zeros((2, BLK, 1, BLK), F32)], axis=2)
        use = (row_slots[child, :, 0] == 0)[:, None, None, None]
        sel = colsel[child, 1:][None, None, :, None]
        head = head + jnp.where(use & (sel == 1), ahead, F32(0)) + jnp.where(use & (sel == 2), blocks, F32(0))
    head = settled(head.reshape(2 * BLK, 4 * BLK), token)
    slabs = []
    for dx in range(4):
        for dl in range(2):
            if dx == 0 and dl == 0:
                slabs.append(head)
                continue
            there = [(r, ((r // 2 - dx) % 4) * 2 + (r + dl) % 2) for r in range(8)]
            slabs.append(lax.ppermute(head, "row", there))
    factor(1, settled(place, head[0, 0]), late)
    factor(2, place, late)
    return tuple(solve(place, source, colsel, strips, inverses, slabs, panel_rows, front, first, rest))


def solution(mesh):
    in_specs = (P("row", "col"), P("row", "col"), P())
    out_specs = (P("row", "col"), P("row", "col"))
    return jax.shard_map(local, mesh=mesh, in_specs=in_specs, out_specs=out_specs, check_vma=False)
```

```python
import functools

import jax
import jax.numpy as jnp
from jax import lax
from jax.experimental import pallas as pl
from jax.experimental.pallas import tpu as pltpu
from jax.sharding import PartitionSpec as P

BLK = 128
PW = 2048
STRIPS = ((0, 1024), (1024, 512), (1536, 512))
STEP = 256
BOTH = ("row", "col")
OFFSETS = (0, -1, 1, 2)
NEAR = 2
F32 = jnp.float32
BF16 = jnp.bfloat16
PARAMS = pltpu.CompilerParams(vmem_limit_bytes=58 << 20)
ANY = pl.BlockSpec(memory_space=pl.ANY)
VMEM = pl.BlockSpec(memory_space=pltpu.VMEM)
SMEM = pl.BlockSpec(memory_space=pltpu.SMEM)


def flat(x, y, z, core):
    return ((x % 4) * 2 + y % 2) * 16 + ((y % 4) // 2) * 8 + (z % 4) * 2 + core % 2


def move(value, *by):
    every = [(x, y, z, c) for x in range(4) for y in range(4) for z in range(4) for c in range(2)]
    pairs = []
    for x, y, z, c in every:
        step = by[c] if len(by) > 1 else by[0]
        if step is not None:
            pairs.append((flat(x, y, z, c), flat(x + step[0], y + step[1], z + step[2], c + step[3])))
    return lax.ppermute(value, BOTH, pairs)


SWAP = (0, 0, 0, 1)


def around(value, *axes):
    out = [value]
    for offset in OFFSETS[1:]:
        out.append(move(value, *[tuple(-offset if n == axis else 0 for n in range(4)) for axis in axes]))
    return out


def held(array, tokens):
    array = lax.optimization_barrier(array)
    ready = functools.reduce(jnp.logical_and, [token <= F32(jnp.finfo(jnp.float32).max) for token in tokens])
    at = (0,) * array.ndim
    return array.at[at].set(jnp.where(ready, array[at], F32(0)))


def gather_leading(corner, y_at, core_at):
    first = core_at == 0
    upper, lower = corner[:BLK], corner[BLK:]
    mine = jnp.where(first, upper, lower)
    other = move(jnp.where(first, lower, upper), SWAP)
    both = jnp.stack([jnp.where(first, mine, other), jnp.where(first, other, mine)])
    own, below, above, opposite = around(both, 1)
    blocks = []
    for y in range(4):
        d = (y - y_at) & 3
        blocks.append(jnp.where(d == 0, own, jnp.where(d == 1, above, jnp.where(d == 2, opposite, below))))
    group = jnp.stack(around(jnp.stack(blocks), 2, 0))
    mine = around(group[:, :2], 0, 2)
    pieces = [*mine, *[move(piece, SWAP) for piece in mine]]
    late = jnp.where(first, move(group[:, 2], SWAP), group[:, 3])
    return pieces, late


def eliminate(tiles):
    tiles = list(tiles)
    count = len(tiles)
    lane = lax.broadcasted_iota(jnp.int32, (8, BLK), 1)
    sub = lax.broadcasted_iota(jnp.int32, (8, BLK), 0)
    upper = []

    def by_lane(x, j):
        return jnp.broadcast_to(x[:, j : j + 1], (8, BLK))

    def by_sub(x, s):
        return jnp.broadcast_to(x[s : s + 1, :], (8, BLK))

    for p in range(count):
        now = tiles[p]
        o = 8 * p
        inside = (lane >= o) & (lane < o + 8)
        column = [by_lane(now, o + t) for t in range(8)]
        a = {(s, t): by_sub(column[t], s) for t in range(8) for s in range(t, 8)}
        rows = [by_sub(now, t) for t in range(8)]
        unit = [jnp.where(lane == o + t, F32(1), jnp.where(inside, F32(0), rows[t])) for t in range(8)]
        r = []
        low = {}
        for t in range(8):
            r.append(lax.rsqrt(a[t, t]))
            for s in range(t + 1, 8):
                low[s, t] = a[s, t] * r[t]
            for u in range(t + 1, 8):
                for s in range(u, 8):
                    a[s, u] = a[s, u] - low[s, t] * low[u, t]
        z = []
        q = []
        for t in range(8):
            z_now, q_now = unit[t], rows[t]
            for s in range(t):
                z_now = z_now - low[t, s] * z[s]
                q_now = q_now - low[t, s] * q[s]
            z.append(z_now * r[t])
            q.append(q_now * r[t])
        y = [None] * 8
        for t in reversed(range(8)):
            y_now = z[t]
            for s in range(t + 1, 8):
                y_now = y_now - low[s, t] * y[s]
            y[t] = y_now * r[t]
        z_tile, q_tile, y_tile = z[0], q[0], y[0]
        for t in range(1, 8):
            z_tile = jnp.where(sub == t, z[t], z_tile)
            q_tile = jnp.where(sub == t, q[t], q_tile)
            y_tile = jnp.where(sub == t, y[t], y_tile)
        upper.append(jnp.where(lane >= o + sub, q_tile, F32(0)))
        tiles[p] = jnp.where(lane <= o + sub, z_tile, F32(0))
        for i in range(p + 1, min(p + 1 + NEAR, count)):
            terms = [by_lane(tiles[i], o + t) * y[t] for t in range(8)]
            while len(terms) > 1:
                terms = [terms[k] + terms[k + 1] for k in range(0, len(terms), 2)]
            tiles[i] = jnp.where(inside, F32(0), tiles[i]) - terms[0]
        far = p + 1 + NEAR
        if far < count:
            zero = jnp.zeros((8, BLK), F32)
            padded = jnp.concatenate([zero] * p + [y_tile] + [zero] * (count - p - 1), axis=0)
            less = exact_nn(jnp.concatenate(tiles[far:], axis=0), padded)
            for i in range(far, count):
                tiles[i] = jnp.where(inside, F32(0), tiles[i]) - less[8 * (i - far) : 8 * (i - far) + 8]
    return tiles, upper


def split(x):
    high = x.astype(BF16)
    return high, (x - high.astype(F32)).astype(BF16)


def dot_nt(a, b):
    return lax.dot_general(a, b, (((1,), (1,)), ((), ())), preferred_element_type=F32)


def dot_nn(a, b):
    return lax.dot_general(a, b, (((1,), (0,)), ((), ())), preferred_element_type=F32)


def pairs(dot, ah, al, bh, bl):
    return dot(ah, bh) + (dot(ah, bl) + dot(al, bh))


def exact_nt(a, b):
    return lax.dot_general(a, b, (((1,), (1,)), ((), ())), precision=lax.Precision.HIGHEST, preferred_element_type=F32)


def exact_nn(a, b):
    return jnp.dot(a, b, precision=lax.Precision.HIGHEST, preferred_element_type=F32)


def offset_of(index):
    return jnp.where(index == 3, 2, jnp.where(index == 2, 1, jnp.where(index == 1, -1, 0)))


def load_leading(place, pieces, late, dest, sems, first_col):
    x, z, core = place[0], place[2], place[3]
    count = dest.shape[0]

    def fetch(source, block_row, block_col):
        pltpu.make_async_copy(
            source,
            dest.at[block_col, pl.ds(pl.multiple_of(block_row * BLK, BLK), BLK), :],
            sems.at[block_col >> 2],
        ).start()

    if late:
        for swapped, ref in enumerate(pieces):
            low_y = (core + swapped) & 1

            def one(n, carry, ref=ref, low_y=low_y):
                far, near, c = n >> 3, (n >> 1) & 3, n & 1
                block_row = ((x + offset_of(near)) & 3) * 2 + low_y + 8
                block_col = 8 + ((z + offset_of(far)) & 3) * 2 + c - first_col

                @pl.when((block_col >= 0) & (block_col < count))
                def _():
                    fetch(ref.at[far, near, c], block_row, block_col)

                return carry

            lax.fori_loop(0, 32, one, 0)
        return
    for number, ref in enumerate(pieces):
        half = (core + number // 4) & 1
        far = OFFSETS[number % 4]

        def one(n, carry, ref=ref, half=half, far=far):
            i, y, c = n >> 2, (n >> 1) & 1, n & 1
            near = offset_of(i)
            dx, dz = jnp.where(half == 0, far, near), jnp.where(half == 0, near, far)
            fetch(ref.at[i, y, c], ((x + dx) & 3) * 2 + y + 8 * half, ((z + dz) & 3) * 2 + c - first_col)
            return carry

        lax.fori_loop(0, 16, one, 0)


def factor_kernel(call, place, *refs):
    start, width = STRIPS[call]
    late = start >= PW // 2
    count = 2 if late else 8
    pieces, refs = refs[:count], refs[count:]
    earlier = refs[: 2 * call]
    out_high, out_low, inv_high, inv_low = refs[2 * call : 4 + 2 * call]
    (lead, high, low, c, diag, inverse, upper, inverse1, low21, load_sem, strip_sem, out_sem) = refs[4 + 2 * call :]
    load_leading(place, pieces, late, lead, load_sem, start // BLK)
    copies = []
    for n in range(call):
        for which, dest in ((0, high), (1, low)):
            copies.append(
                pltpu.make_async_copy(
                    earlier[2 * n + which].at[pl.ds(start - STRIPS[n][0], PW - start), :],
                    dest.at[:, pl.ds(*STRIPS[n])],
                    strip_sem.at[2 * n + which],
                )
            )
    for copy in copies:
        copy.start()

    def wait_lead(n):
        loaded = lead.at[4 * n : 4 * n + 4, PW // 2 if late else 0 :, :]
        pltpu.make_async_copy(loaded, loaded, load_sem.at[n]).wait()

    def outs(kk):
        rows, cols = pl.ds(STEP * kk, PW - start - STEP * kk), pl.ds(STEP * kk, STEP)
        source = pl.ds(start + STEP * kk, STEP)
        return [
            pltpu.make_async_copy(high.at[rows, source], out_high.at[rows, cols], out_sem.at[2 * kk]),
            pltpu.make_async_copy(low.at[rows, source], out_low.at[rows, cols], out_sem.at[2 * kk + 1]),
        ]

    wait_lead(0)
    for copy in copies:
        copy.wait()

    def put(rows, cols, value):
        h, l = split(value)
        high[rows, cols] = h
        low[rows, cols] = l

    def under(at, tile):
        wide = (PW - start - at) // 512

        def one(t, carry):
            tile(pl.multiple_of(at + t * 512, STEP), 512)
            return carry

        lax.fori_loop(0, wide, one, 0)
        if at + wide * 512 < PW - start:
            tile(at + wide * 512, STEP)

    def before(kk):
        if kk and kk % 2 == 0:
            wait_lead(kk // 2)
        known = start + STEP * kk
        r0 = STEP * kk

        def tile(at, size):
            rows = pl.ds(at, size)
            whole = pl.ds(pl.multiple_of(start + at, STEP), size)
            value = jnp.concatenate([lead[2 * kk, whole, :], lead[2 * kk + 1, whole, :]], axis=1)
            if known > 0:
                value = value - pairs(
                    dot_nt, high[rows, :known], low[rows, :known], high[r0 : r0 + STEP, :known], low[r0 : r0 + STEP, :known]
                )
            c[rows, :] = value

        tile(r0, STEP)
        under(r0 + STEP, tile)
        diag[...] = c[r0 : r0 + BLK, :BLK]

    def between(kk):
        r0 = STEP * kk
        col = start + r0
        w1 = inverse[...]
        l21 = exact_nt(c[r0 + BLK : r0 + STEP, :BLK], w1)
        diag[...] = c[r0 + BLK : r0 + STEP, BLK:] - exact_nt(l21, l21)
        inverse1[...] = w1
        low21[...] = l21
        put(pl.ds(r0, BLK), pl.ds(col, BLK), upper[...].T)
        put(pl.ds(r0, BLK), pl.ds(col + BLK, BLK), jnp.zeros((BLK, BLK), F32))
        put(pl.ds(r0 + BLK, BLK), pl.ds(col, BLK), l21)

    def after(kk):
        r0 = STEP * kk
        col = start + r0
        w2 = inverse[...]
        put(pl.ds(r0 + BLK, BLK), pl.ds(col + BLK, BLK), upper[...].T)
        w21 = -exact_nn(w2, exact_nn(low21[...], inverse1[...]))
        top = jnp.concatenate([inverse1[...], jnp.zeros((BLK, BLK), F32)], axis=1)
        w = jnp.concatenate([top, jnp.concatenate([w21, w2], axis=1)], axis=0)
        wh, wl = split(w)
        inv_high[kk] = wh
        inv_low[kk] = wl

        def tile(at, size):
            rows = pl.ds(at, size)
            ch, cl = split(c[rows, :])
            put(rows, pl.ds(col, STEP), pairs(dot_nt, ch, cl, inv_high[kk], inv_low[kk]))

        under(r0 + STEP, tile)
        for copy in outs(kk):
            copy.start()

    def half(h, carry):
        for kk in range(width // STEP):
            pl.when(h == 2 * kk)(functools.partial(before, kk))
        w, u = eliminate([diag[8 * i : 8 * i + 8, :] for i in range(16)])
        for i in range(16):
            inverse[8 * i : 8 * i + 8, :] = w[i]
            upper[8 * i : 8 * i + 8, :] = u[i]
        for kk in range(width // STEP):
            pl.when(h == 2 * kk)(functools.partial(between, kk))
            pl.when(h == 2 * kk + 1)(functools.partial(after, kk))
        return carry

    lax.fori_loop(0, width // BLK, half, 0)
    for kk in range(width // STEP):
        for copy in outs(kk):
            copy.wait()


def factor_strip(call, place, pieces, earlier):
    start, width = STRIPS[call]
    rows = PW - start
    known = start + width
    strip = jax.ShapeDtypeStruct((rows, width), BF16)
    inverses = jax.ShapeDtypeStruct((width // STEP, STEP, STEP), BF16)
    block = pltpu.VMEM((BLK, BLK), F32)
    return pl.pallas_call(
        functools.partial(factor_kernel, call),
        out_shape=[strip, strip, inverses, inverses],
        in_specs=[SMEM] + [ANY] * (len(pieces) + 2 * call),
        out_specs=[ANY, ANY, VMEM, VMEM],
        scratch_shapes=[
            pltpu.VMEM((width // BLK, PW, BLK), F32),
            pltpu.VMEM((rows, known), BF16),
            pltpu.VMEM((rows, known), BF16),
            pltpu.VMEM((rows, STEP), F32),
            block,
            block,
            block,
            block,
            block,
            pltpu.SemaphoreType.DMA((width // 512,)),
            pltpu.SemaphoreType.DMA((max(2 * call, 1),)),
            pltpu.SemaphoreType.DMA((2 * width // STEP,)),
        ],
        compiler_params=PARAMS,
        cost_estimate=pl.CostEstimate(flops=int(7e7) * width, bytes_accessed=int(1e8), transcendentals=0),
        name=f"factor{call}",
    )(place, *pieces, *earlier)


def head_kernel(hit, colsel, token, front, f0, f1, g0, g1, own, below, above, opposite, head, late, sems):
    del token
    copies = [pltpu.make_async_copy(ref, late.at[n], sems.at[n]) for n, ref in enumerate((own, below, above, opposite))]
    for copy in copies:
        copy.start()
    for w in range(2):
        rows = slice(w * BLK, (w + 1) * BLK)
        for n in range(1, 5):
            total = front[rows, n * BLK : (n + 1) * BLK]
            for k, (first, rest) in enumerate(((f0, g0), (f1, g1))):
                for sel, j in ((1, n), (2, n - 1)):
                    if j < 4:
                        block = first[0, w] if j == 0 else rest[0, w, :, (j - 1) * BLK : j * BLK]
                        use = (hit[k, w] == 1) & (colsel[k, n] == sel)
                        total = total + jnp.where(use, block, F32(0))
            head[rows, (n - 1) * BLK : n * BLK] = total
    for copy in copies:
        copy.wait()


def head_rows(hit, colsel, token, front, first, rest, late):
    cols = front.shape[1]

    def child(k):
        return lambda i: (4 * k, 0, 0, 0)

    return pl.pallas_call(
        head_kernel,
        grid=(1,),
        out_shape=[
            jax.ShapeDtypeStruct((2 * BLK, cols - BLK), F32),
            jax.ShapeDtypeStruct((4, *late[0].shape), F32),
        ],
        in_specs=[
            SMEM,
            SMEM,
            ANY,
            pl.BlockSpec((2 * BLK, cols), lambda i: (0, 0)),
            pl.BlockSpec((1, 2, BLK, BLK), child(0)),
            pl.BlockSpec((1, 2, BLK, BLK), child(1)),
            pl.BlockSpec((1, 2, BLK, 3 * BLK), child(0)),
            pl.BlockSpec((1, 2, BLK, 3 * BLK), child(1)),
            ANY,
            ANY,
            ANY,
            ANY,
        ],
        out_specs=[pl.BlockSpec((2 * BLK, cols - BLK), lambda i: (0, 0)), ANY],
        scratch_shapes=[pltpu.SemaphoreType.DMA((4,))],
        compiler_params=PARAMS,
        name="head",
    )(hit, colsel, token, front, first, first, rest, rest, *late)


def solve_kernel(place, source, colsel, *refs):
    n_strips = 2 * len(STRIPS)
    strips, inverses, refs = refs[:n_strips], refs[n_strips : 2 * n_strips], refs[2 * n_strips :]
    slabs, refs = refs[:8], refs[8:]
    panel_rows, front, first, rest, panel_out, trailing = refs[:6]
    high, low, xh, xl, yh, yl, raw, yraw, base, child, sems, raw_sem, slab_sem, child_sem = refs[6:]
    x, y, z, core = place[0], place[1], place[2], place[3]
    row = x * 2 + y % 2
    col = (y // 2) * 8 + z * 2 + core
    blocks = PW // STEP
    factor_rows = [[] for _ in range(blocks)]
    for k in range(blocks):
        for n, (start, width) in enumerate(STRIPS):
            if start <= STEP * k:
                cols = min(width, STEP * (k + 1) - start)
                for which, dest in ((0, high), (1, low)):
                    factor_rows[k].append(
                        pltpu.make_async_copy(
                            strips[2 * n + which].at[pl.ds(STEP * k - start, STEP), pl.ds(0, cols)],
                            dest.at[pl.ds(STEP * k, STEP), pl.ds(start, cols)],
                            sems.at[k, 2 * n + which],
                        )
                    )

    def start_all(copies):
        for copy in copies:
            copy.start()

    raws = [pltpu.make_async_copy(panel_rows.at[pl.ds(4 * n, 4)], raw.at[pl.ds(4 * n, 4)], raw_sem.at[n]) for n in range(4)]
    slab_copies = []
    for dx in range(4):
        for dl in range(2):
            there = ((x + dx) % 4) * 2 + (y + dl) % 2
            for second in range(2):
                at = pl.multiple_of((there + 8 * second) * BLK, BLK)
                slab_copies.append(
                    pltpu.make_async_copy(
                        slabs[dx * 2 + dl].at[pl.ds(second * BLK, BLK), :],
                        yraw.at[pl.ds(at, BLK), :],
                        slab_sem.at[(dx * 2 + dl) * 2 + second],
                    )
                )
    children = [
        pltpu.make_async_copy(front.at[2 * BLK :, BLK:], base, child_sem.at[0]),
        pltpu.make_async_copy(first, child.at[:, :, :, pl.ds(0, BLK)], child_sem.at[1]),
        pltpu.make_async_copy(rest, child.at[:, :, :, pl.ds(BLK, 3 * BLK)], child_sem.at[2]),
    ]
    start_all(slab_copies)
    raws[0].start()
    for k in range(3):
        start_all(factor_rows[k])
    for copy in slab_copies:
        copy.wait()
    panel_out[: 2 * BLK, :] = jnp.zeros((2 * BLK, BLK), F32)
    for k in range(PW // STEP):
        known = STEP * k
        if k % 2 == 0:
            raws[k // 2].wait()
            if k // 2 + 1 < len(raws):
                raws[k // 2 + 1].start()
        if k + 3 < blocks:
            start_all(factor_rows[k + 3])
        if k == 5:
            start_all(children)
        for copy in factor_rows[k]:
            copy.wait()
        strip = max(n for n, (start, _) in enumerate(STRIPS) if start <= known)
        wh, wl = inverses[2 * strip], inverses[2 * strip + 1]
        inner = k - STRIPS[strip][0] // STEP
        here = slice(known, known + STEP)
        value = yraw[here, :]
        if k:
            value = value - pairs(dot_nn, high[here, :known], low[here, :known], yh[:known, :], yl[:known, :])
        vh, vl = split(value)
        got = pairs(dot_nn, wh[inner], wl[inner], vh, vl)
        yh[here, :], yl[here, :] = split(got)

        def tile(t, carry, k=k, known=known, here=here, wh=wh, wl=wl, inner=inner):
            rows = pl.ds(pl.multiple_of(t * 512, 512), 512)
            value = jnp.concatenate([raw[2 * k, rows, :], raw[2 * k + 1, rows, :]], axis=1)
            if k:
                value = value - pairs(dot_nt, xh[rows, :known], xl[rows, :known], high[here, :known], low[here, :known])
            vh, vl = split(value)
            got = pairs(dot_nt, vh, vl, wh[inner], wl[inner])
            xh[rows, here], xl[rows, here] = split(got)
            for side in range(2):

                @pl.when(col == 2 * k + side)
                def _():
                    panel_out[pl.ds(pl.multiple_of(2 * BLK + t * 512, BLK), 512), :] = got[:, side * BLK : (side + 1) * BLK]

            return carry

        lax.fori_loop(0, raw.shape[1] // 512, tile, 0)
    lanes = pl.ds(pl.multiple_of(col * BLK, BLK), BLK)
    for second in range(2):
        block_row = row + 8 * second

        @pl.when(block_row >= col)
        def _():
            rows = pl.ds(pl.multiple_of(block_row * BLK, BLK), BLK)
            panel_out[second * BLK : (second + 1) * BLK, :] = high[rows, lanes].astype(F32) + low[rows, lanes].astype(F32)

    trailing[: 2 * BLK, :] = jnp.zeros((2 * BLK, trailing.shape[1]), F32)
    trailing[:, :BLK] = jnp.zeros((trailing.shape[0], BLK), F32)

    for copy in children:
        copy.wait()

    def assemble(q, carry):
        rows = pl.ds(pl.multiple_of(q * BLK, BLK), BLK)
        out = pl.ds(pl.multiple_of((q + 2) * BLK, BLK), BLK)
        for n in range(1, 5):
            total = base[rows, (n - 1) * BLK : n * BLK]
            for k in range(2):
                at = source[k, q + 2]
                use = at >= 0
                at = jnp.maximum(at, 0)
                for sel, j in ((1, n), (2, n - 1)):
                    if j < 4:
                        block = child[at, q & 1, :, j * BLK : (j + 1) * BLK]
                        total = total + jnp.where(use & (colsel[k, n] == sel), block, F32(0))
            trailing[out, n * BLK : (n + 1) * BLK] = total
        return carry

    lax.fori_loop(0, 8, assemble, 0)

    def update(t, carry):
        rows = pl.ds(pl.multiple_of(t * 512, 512), 512)
        out = pl.ds(pl.multiple_of(2 * BLK + t * 512, STEP), 512)
        trailing[out, BLK:] = trailing[out, BLK:] - pairs(dot_nn, xh[rows, :], xl[rows, :], yh[...], yl[...])
        return carry

    lax.fori_loop(0, raw.shape[1] // 512, update, 0)


def solve(place, source, colsel, strips, inverses, slabs, panel_rows, front, first, rest):
    rows, cols = front.shape
    under = rows - 2 * BLK
    return pl.pallas_call(
        solve_kernel,
        out_shape=[jax.ShapeDtypeStruct((rows, BLK), F32), jax.ShapeDtypeStruct((rows, cols), F32)],
        in_specs=[SMEM] * 3 + [ANY] * len(strips) + [VMEM] * len(inverses) + [ANY] * 12,
        out_specs=[VMEM, VMEM],
        scratch_shapes=[
            pltpu.VMEM((PW, PW), BF16),
            pltpu.VMEM((PW, PW), BF16),
            pltpu.VMEM((under, PW), BF16),
            pltpu.VMEM((under, PW), BF16),
            pltpu.VMEM((PW, cols - BLK), BF16),
            pltpu.VMEM((PW, cols - BLK), BF16),
            pltpu.VMEM((16, under, BLK), F32),
            pltpu.VMEM((PW, cols - BLK), F32),
            pltpu.VMEM((under, cols - BLK), F32),
            pltpu.VMEM((8, 2, BLK, 4 * BLK), F32),
            pltpu.SemaphoreType.DMA((PW // STEP, len(strips))),
            pltpu.SemaphoreType.DMA((4,)),
            pltpu.SemaphoreType.DMA((16,)),
            pltpu.SemaphoreType.DMA((3,)),
        ],
        compiler_params=PARAMS,
        name="solve",
    )(place, source, colsel, *strips, *inverses, *slabs, panel_rows, front, first, rest)


def local(front, updates, maps):
    row_at = lax.axis_index("row")
    col_at = lax.axis_index("col")
    place = jnp.stack([row_at // 2, (col_at // 8) * 2 + row_at % 2, (col_at // 2) % 4, col_at % 2]).astype(jnp.int32)
    slots = maps >> 4
    row_slots = lax.dynamic_index_in_dim(slots.reshape(2, 2, 8, 4), row_at, 2, keepdims=False)
    col_slots = lax.dynamic_index_in_dim(slots.reshape(2, 16, 4), col_at, 1, keepdims=False)

    slot = jnp.arange(5)
    own = jnp.pad(row_slots, ((0, 0), (0, 0), (0, 1)), constant_values=-1) == slot
    prior = jnp.pad(row_slots, ((0, 0), (0, 0), (1, 0)), constant_values=-1) == slot
    source = jnp.where(own, slot, jnp.where(prior, slot - 1, -8)) + 4 * jnp.arange(2)[:, None, None]
    source = source.transpose(0, 2, 1).reshape(2, 10).astype(jnp.int32)
    own = jnp.pad(col_slots, ((0, 0), (0, 1)), constant_values=-1) == slot
    prior = jnp.pad(col_slots, ((0, 0), (1, 0)), constant_values=-1) == slot
    colsel = jnp.where(own, 1, jnp.where(prior, 2, 0)).astype(jnp.int32)

    def outgoing(part):
        return part.reshape(2, 8, BLK, part.shape[1]).transpose(1, 0, 2, 3)

    def exchange(outgoing):
        return lax.all_to_all(outgoing, "row", split_axis=0, concat_axis=0, tiled=True)

    first = exchange(outgoing(updates[:, :BLK]))
    meets = col_slots[:, 0] == 0
    panel = front[:, :BLK].reshape(5, 2, BLK, BLK)
    parts = []
    for m in range(5):
        total = panel[m]
        for child in range(2):
            for a in (m, m - 1):
                if 0 <= a < 4:
                    hit = (row_slots[child, :, a] == m) & meets[child]
                    total = total + jnp.where(hit[:, None, None], first[4 * child + a], F32(0))
        parts.append(total)
    corner = parts[0].reshape(2 * BLK, BLK)
    under = jnp.stack(parts[1:]).reshape(8 * BLK, BLK)
    pieces, late = gather_leading(corner, place[1], place[3])

    tokens = [piece[0, 0, 0, 0, 0] for piece in pieces[5:]]
    panel_rows = lax.all_gather(held(under, tokens), "col", axis=0, tiled=True).reshape(16, 8 * BLK, BLK)
    late = around(held(late, tokens), 2)
    rest = exchange(held(outgoing(updates[:, BLK:]), tokens))

    strips, inverses = [], []

    def factor(call, place, pieces):
        got = factor_strip(call, place, pieces, strips)
        strips.extend(got[:2])
        inverses.extend(got[2:])

    factor(0, place, pieces)
    hit = (row_slots[:, :, 0] == 0).astype(jnp.int32)
    head, late = head_rows(hit, colsel, inverses[0], front, first, rest, late)
    late = [late, move(late, SWAP)]
    slabs = []
    for dx in range(4):
        for dl in range(2):
            if dx == 0 and dl == 0:
                slabs.append(head)
                continue
            there = [(r, ((r // 2 - dx) % 4) * 2 + (r + dl) % 2) for r in range(8)]
            slabs.append(lax.ppermute(head, "row", there))
    factor(1, place, late)
    factor(2, place, late)
    return tuple(solve(place, source, colsel, strips, inverses, slabs, panel_rows, front, first, rest))


def solution(mesh):
    in_specs = (P("row", "col"), P("row", "col"), P())
    out_specs = (P("row", "col"), P("row", "col"))
    return jax.shard_map(local, mesh=mesh, in_specs=in_specs, out_specs=out_specs, check_vma=False)
```

```python
import functools

import jax
import jax.numpy as jnp
from jax import lax
from jax.experimental import pallas as pl
from jax.experimental.pallas import tpu as pltpu
from jax.sharding import PartitionSpec as P

BLK = 128
PW = 2048
STRIPS = ((0, 1024), (1024, 512), (1536, 512))
STEP = 256
BOTH = ("row", "col")
OFFSETS = (0, -1, 1, 2)
NEAR = 2
F32 = jnp.float32
BF16 = jnp.bfloat16
PARAMS = pltpu.CompilerParams(vmem_limit_bytes=58 << 20)
ANY = pl.BlockSpec(memory_space=pl.ANY)
VMEM = pl.BlockSpec(memory_space=pltpu.VMEM)
SMEM = pl.BlockSpec(memory_space=pltpu.SMEM)


def flat(x, y, z, core):
    return ((x % 4) * 2 + y % 2) * 16 + ((y % 4) // 2) * 8 + (z % 4) * 2 + core % 2


def move(value, *by):
    every = [(x, y, z, c) for x in range(4) for y in range(4) for z in range(4) for c in range(2)]
    pairs = []
    for x, y, z, c in every:
        step = by[c] if len(by) > 1 else by[0]
        if step is not None:
            pairs.append((flat(x, y, z, c), flat(x + step[0], y + step[1], z + step[2], c + step[3])))
    return lax.ppermute(value, BOTH, pairs)


SWAP = (0, 0, 0, 1)


def around(value, *axes):
    out = [value]
    for offset in OFFSETS[1:]:
        out.append(move(value, *[tuple(-offset if n == axis else 0 for n in range(4)) for axis in axes]))
    return out


def held(array, tokens):
    array = lax.optimization_barrier(array)
    ready = functools.reduce(jnp.logical_and, [token <= F32(jnp.finfo(jnp.float32).max) for token in tokens])
    at = (0,) * array.ndim
    first = jnp.where(ready, array[at], F32(0)).reshape((1,) * array.ndim)
    return lax.dynamic_update_slice(array, first, at)


def gather_leading(corner, y_at, core_at):
    first = core_at == 0
    upper, lower = corner[:BLK], corner[BLK:]
    mine = jnp.where(first, upper, lower)
    other = move(jnp.where(first, lower, upper), SWAP)
    both = jnp.stack([jnp.where(first, mine, other), jnp.where(first, other, mine)])
    own, below, above, opposite = around(both, 1)
    blocks = []
    for y in range(4):
        d = (y - y_at) & 3
        blocks.append(jnp.where(d == 0, own, jnp.where(d == 1, above, jnp.where(d == 2, opposite, below))))
    group = jnp.stack(around(jnp.stack(blocks), 2, 0))
    mine = around(group[:, :2], 0, 2)
    pieces = [*mine, *[move(piece, SWAP) for piece in mine]]
    late = jnp.where(first, move(group[:, 2], SWAP), group[:, 3])
    return pieces, late


def eliminate(tiles):
    tiles = list(tiles)
    count = len(tiles)
    lane = lax.broadcasted_iota(jnp.int32, (8, BLK), 1)
    sub = lax.broadcasted_iota(jnp.int32, (8, BLK), 0)
    upper = []

    def by_lane(x, j):
        return jnp.broadcast_to(x[:, j : j + 1], (8, BLK))

    def by_sub(x, s):
        return jnp.broadcast_to(x[s : s + 1, :], (8, BLK))

    for p in range(count):
        now = tiles[p]
        o = 8 * p
        inside = (lane >= o) & (lane < o + 8)
        column = [by_lane(now, o + t) for t in range(8)]
        a = {(s, t): by_sub(column[t], s) for t in range(8) for s in range(t, 8)}
        rows = [by_sub(now, t) for t in range(8)]
        unit = [jnp.where(lane == o + t, F32(1), jnp.where(inside, F32(0), rows[t])) for t in range(8)]
        r = []
        low = {}
        for t in range(8):
            r.append(lax.rsqrt(a[t, t]))
            for s in range(t + 1, 8):
                low[s, t] = a[s, t] * r[t]
            for u in range(t + 1, 8):
                for s in range(u, 8):
                    a[s, u] = a[s, u] - low[s, t] * low[u, t]
        z = []
        q = []
        for t in range(8):
            z_now, q_now = unit[t], rows[t]
            for s in range(t):
                z_now = z_now - low[t, s] * z[s]
                q_now = q_now - low[t, s] * q[s]
            z.append(z_now * r[t])
            q.append(q_now * r[t])
        y = [None] * 8
        for t in reversed(range(8)):
            y_now = z[t]
            for s in range(t + 1, 8):
                y_now = y_now - low[s, t] * y[s]
            y[t] = y_now * r[t]
        z_tile, q_tile, y_tile = z[0], q[0], y[0]
        for t in range(1, 8):
            z_tile = jnp.where(sub == t, z[t], z_tile)
            q_tile = jnp.where(sub == t, q[t], q_tile)
            y_tile = jnp.where(sub == t, y[t], y_tile)
        upper.append(jnp.where(lane >= o + sub, q_tile, F32(0)))
        tiles[p] = jnp.where(lane <= o + sub, z_tile, F32(0))
        for i in range(p + 1, min(p + 1 + NEAR, count)):
            terms = [by_lane(tiles[i], o + t) * y[t] for t in range(8)]
            while len(terms) > 1:
                terms = [terms[k] + terms[k + 1] for k in range(0, len(terms), 2)]
            tiles[i] = jnp.where(inside, F32(0), tiles[i]) - terms[0]
        far = p + 1 + NEAR
        if far < count:
            zero = jnp.zeros((8, BLK), F32)
            padded = jnp.concatenate([zero] * p + [y_tile] + [zero] * (count - p - 1), axis=0)
            less = exact_nn(jnp.concatenate(tiles[far:], axis=0), padded)
            for i in range(far, count):
                tiles[i] = jnp.where(inside, F32(0), tiles[i]) - less[8 * (i - far) : 8 * (i - far) + 8]
    return tiles, upper


def split(x):
    high = x.astype(BF16)
    return high, (x - high.astype(F32)).astype(BF16)


def dot_nt(a, b):
    return lax.dot_general(a, b, (((1,), (1,)), ((), ())), preferred_element_type=F32)


def dot_nn(a, b):
    return lax.dot_general(a, b, (((1,), (0,)), ((), ())), preferred_element_type=F32)


def pairs(dot, ah, al, bh, bl):
    return dot(ah, bh) + (dot(ah, bl) + dot(al, bh))


def exact_nt(a, b):
    return lax.dot_general(a, b, (((1,), (1,)), ((), ())), precision=lax.Precision.HIGHEST, preferred_element_type=F32)


def exact_nn(a, b):
    return jnp.dot(a, b, precision=lax.Precision.HIGHEST, preferred_element_type=F32)


def offset_of(index):
    return jnp.where(index == 3, 2, jnp.where(index == 2, 1, jnp.where(index == 1, -1, 0)))


def load_leading(place, pieces, late, dest, sems, first_col):
    x, z, core = place[0], place[2], place[3]
    count = dest.shape[0]

    def fetch(source, block_row, block_col):
        pltpu.make_async_copy(
            source,
            dest.at[block_col, pl.ds(pl.multiple_of(block_row * BLK, BLK), BLK), :],
            sems.at[block_col >> 2],
        ).start()

    if late:
        for swapped, ref in enumerate(pieces):
            low_y = (core + swapped) & 1

            def one(n, carry, ref=ref, low_y=low_y):
                far, near, c = n >> 3, (n >> 1) & 3, n & 1
                block_row = ((x + offset_of(near)) & 3) * 2 + low_y + 8
                block_col = 8 + ((z + offset_of(far)) & 3) * 2 + c - first_col

                @pl.when((block_col >= 0) & (block_col < count))
                def _():
                    fetch(ref.at[far, near, c], block_row, block_col)

                return carry

            lax.fori_loop(0, 32, one, 0)
        return
    for number, ref in enumerate(pieces):
        half = (core + number // 4) & 1
        far = OFFSETS[number % 4]

        def one(n, carry, ref=ref, half=half, far=far):
            i, y, c = n >> 2, (n >> 1) & 1, n & 1
            near = offset_of(i)
            dx, dz = jnp.where(half == 0, far, near), jnp.where(half == 0, near, far)
            fetch(ref.at[i, y, c], ((x + dx) & 3) * 2 + y + 8 * half, ((z + dz) & 3) * 2 + c - first_col)
            return carry

        lax.fori_loop(0, 16, one, 0)


def factor_kernel(call, place, *refs):
    start, width = STRIPS[call]
    late = start >= PW // 2
    count = 2 if late else 8
    pieces, refs = refs[:count], refs[count:]
    earlier = refs[: 2 * call]
    out_high, out_low, inv_high, inv_low = refs[2 * call : 4 + 2 * call]
    (lead, high, low, c, diag, inverse, upper, inverse1, low21, load_sem, strip_sem, out_sem) = refs[4 + 2 * call :]
    load_leading(place, pieces, late, lead, load_sem, start // BLK)
    copies = []
    for n in range(call):
        for which, dest in ((0, high), (1, low)):
            copies.append(
                pltpu.make_async_copy(
                    earlier[2 * n + which].at[pl.ds(start - STRIPS[n][0], PW - start), :],
                    dest.at[:, pl.ds(*STRIPS[n])],
                    strip_sem.at[2 * n + which],
                )
            )
    for copy in copies:
        copy.start()

    def wait_lead(n):
        loaded = lead.at[4 * n : 4 * n + 4, PW // 2 if late else 0 :, :]
        pltpu.make_async_copy(loaded, loaded, load_sem.at[n]).wait()

    def outs(kk):
        rows, cols = pl.ds(STEP * kk, PW - start - STEP * kk), pl.ds(STEP * kk, STEP)
        source = pl.ds(start + STEP * kk, STEP)
        return [
            pltpu.make_async_copy(high.at[rows, source], out_high.at[rows, cols], out_sem.at[2 * kk]),
            pltpu.make_async_copy(low.at[rows, source], out_low.at[rows, cols], out_sem.at[2 * kk + 1]),
        ]

    wait_lead(0)
    for copy in copies:
        copy.wait()

    def put(rows, cols, value):
        h, l = split(value)
        high[rows, cols] = h
        low[rows, cols] = l

    def under(at, tile):
        wide = (PW - start - at) // 512

        def one(t, carry):
            tile(pl.multiple_of(at + t * 512, STEP), 512)
            return carry

        lax.fori_loop(0, wide, one, 0)
        if at + wide * 512 < PW - start:
            tile(at + wide * 512, STEP)

    def before(kk):
        if kk and kk % 2 == 0:
            wait_lead(kk // 2)
        known = start + STEP * kk
        r0 = STEP * kk

        def tile(at, size):
            rows = pl.ds(at, size)
            whole = pl.ds(pl.multiple_of(start + at, STEP), size)
            value = jnp.concatenate([lead[2 * kk, whole, :], lead[2 * kk + 1, whole, :]], axis=1)
            if known > 0:
                value = value - pairs(
                    dot_nt, high[rows, :known], low[rows, :known], high[r0 : r0 + STEP, :known], low[r0 : r0 + STEP, :known]
                )
            c[rows, :] = value

        tile(r0, STEP)
        under(r0 + STEP, tile)
        diag[...] = c[r0 : r0 + BLK, :BLK]

    def between(kk):
        r0 = STEP * kk
        col = start + r0
        w1 = inverse[...]
        l21 = exact_nt(c[r0 + BLK : r0 + STEP, :BLK], w1)
        diag[...] = c[r0 + BLK : r0 + STEP, BLK:] - exact_nt(l21, l21)
        inverse1[...] = w1
        low21[...] = l21
        put(pl.ds(r0, BLK), pl.ds(col, BLK), upper[...].T)
        put(pl.ds(r0, BLK), pl.ds(col + BLK, BLK), jnp.zeros((BLK, BLK), F32))
        put(pl.ds(r0 + BLK, BLK), pl.ds(col, BLK), l21)

    def after(kk):
        r0 = STEP * kk
        col = start + r0
        w2 = inverse[...]
        put(pl.ds(r0 + BLK, BLK), pl.ds(col + BLK, BLK), upper[...].T)
        w21 = -exact_nn(w2, exact_nn(low21[...], inverse1[...]))
        top = jnp.concatenate([inverse1[...], jnp.zeros((BLK, BLK), F32)], axis=1)
        w = jnp.concatenate([top, jnp.concatenate([w21, w2], axis=1)], axis=0)
        wh, wl = split(w)
        inv_high[kk] = wh
        inv_low[kk] = wl

        def tile(at, size):
            rows = pl.ds(at, size)
            ch, cl = split(c[rows, :])
            put(rows, pl.ds(col, STEP), pairs(dot_nt, ch, cl, inv_high[kk], inv_low[kk]))

        under(r0 + STEP, tile)
        for copy in outs(kk):
            copy.start()

    def half(h, carry):
        for kk in range(width // STEP):
            pl.when(h == 2 * kk)(functools.partial(before, kk))
        w, u = eliminate([diag[8 * i : 8 * i + 8, :] for i in range(16)])
        for i in range(16):
            inverse[8 * i : 8 * i + 8, :] = w[i]
            upper[8 * i : 8 * i + 8, :] = u[i]
        for kk in range(width // STEP):
            pl.when(h == 2 * kk)(functools.partial(between, kk))
            pl.when(h == 2 * kk + 1)(functools.partial(after, kk))
        return carry

    lax.fori_loop(0, width // BLK, half, 0)
    for kk in range(width // STEP):
        for copy in outs(kk):
            copy.wait()


def factor_strip(call, place, pieces, earlier):
    start, width = STRIPS[call]
    rows = PW - start
    known = start + width
    strip = jax.ShapeDtypeStruct((rows, width), BF16)
    inverses = jax.ShapeDtypeStruct((width // STEP, STEP, STEP), BF16)
    block = pltpu.VMEM((BLK, BLK), F32)
    return pl.pallas_call(
        functools.partial(factor_kernel, call),
        out_shape=[strip, strip, inverses, inverses],
        in_specs=[SMEM] + [ANY] * (len(pieces) + 2 * call),
        out_specs=[ANY, ANY, VMEM, VMEM],
        scratch_shapes=[
            pltpu.VMEM((width // BLK, PW, BLK), F32),
            pltpu.VMEM((rows, known), BF16),
            pltpu.VMEM((rows, known), BF16),
            pltpu.VMEM((rows, STEP), F32),
            block,
            block,
            block,
            block,
            block,
            pltpu.SemaphoreType.DMA((width // 512,)),
            pltpu.SemaphoreType.DMA((max(2 * call, 1),)),
            pltpu.SemaphoreType.DMA((2 * width // STEP,)),
        ],
        compiler_params=PARAMS,
        cost_estimate=pl.CostEstimate(flops=int(7e7) * width, bytes_accessed=int(1e8), transcendentals=0),
        name=f"factor{call}",
    )(place, *pieces, *earlier)


def head_kernel(hit, colsel, token, front, f0, f1, g0, g1, own, below, above, opposite, head, late):
    del token
    for n, ref in enumerate((own, below, above, opposite)):
        late[n] = ref[...]
    for w in range(2):
        rows = slice(w * BLK, (w + 1) * BLK)
        for n in range(1, 5):
            total = front[rows, n * BLK : (n + 1) * BLK]
            for k, (first, rest) in enumerate(((f0, g0), (f1, g1))):
                for sel, j in ((1, n), (2, n - 1)):
                    if j < 4:
                        block = first[0, w] if j == 0 else rest[0, w, :, (j - 1) * BLK : j * BLK]
                        use = (hit[k, w] == 1) & (colsel[k, n] == sel)
                        total = total + jnp.where(use, block, F32(0))
            head[rows, (n - 1) * BLK : n * BLK] = total


def head_rows(hit, colsel, token, front, first, rest, late):
    cols = front.shape[1]

    def child(k):
        return lambda i: (4 * k, 0, 0, 0)

    return pl.pallas_call(
        head_kernel,
        grid=(1,),
        out_shape=[
            jax.ShapeDtypeStruct((2 * BLK, cols - BLK), F32),
            jax.ShapeDtypeStruct((4, *late[0].shape), F32),
        ],
        in_specs=[
            SMEM,
            SMEM,
            ANY,
            pl.BlockSpec((2 * BLK, cols), lambda i: (0, 0)),
            pl.BlockSpec((1, 2, BLK, BLK), child(0)),
            pl.BlockSpec((1, 2, BLK, BLK), child(1)),
            pl.BlockSpec((1, 2, BLK, 3 * BLK), child(0)),
            pl.BlockSpec((1, 2, BLK, 3 * BLK), child(1)),
            VMEM,
            VMEM,
            VMEM,
            VMEM,
        ],
        out_specs=[pl.BlockSpec((2 * BLK, cols - BLK), lambda i: (0, 0)), VMEM],
        compiler_params=PARAMS,
        name="head",
    )(hit, colsel, token, front, first, first, rest, rest, *late)


def solve_kernel(place, source, colsel, *refs):
    n_strips = 2 * len(STRIPS)
    strips, inverses, refs = refs[:n_strips], refs[n_strips : 2 * n_strips], refs[2 * n_strips :]
    slabs, refs = refs[:8], refs[8:]
    panel_rows, front, first, rest, panel_out, trailing = refs[:6]
    high, low, xh, xl, yh, yl, raw, yraw, base, child, sems, raw_sem, slab_sem, child_sem = refs[6:]
    x, y, z, core = place[0], place[1], place[2], place[3]
    row = x * 2 + y % 2
    col = (y // 2) * 8 + z * 2 + core
    blocks = PW // STEP
    factor_rows = [[] for _ in range(blocks)]
    for k in range(blocks):
        for n, (start, width) in enumerate(STRIPS):
            if start <= STEP * k:
                cols = min(width, STEP * (k + 1) - start)
                for which, dest in ((0, high), (1, low)):
                    factor_rows[k].append(
                        pltpu.make_async_copy(
                            strips[2 * n + which].at[pl.ds(STEP * k - start, STEP), pl.ds(0, cols)],
                            dest.at[pl.ds(STEP * k, STEP), pl.ds(start, cols)],
                            sems.at[k, 2 * n + which],
                        )
                    )

    def start_all(copies):
        for copy in copies:
            copy.start()

    raws = [pltpu.make_async_copy(panel_rows.at[pl.ds(4 * n, 4)], raw.at[pl.ds(4 * n, 4)], raw_sem.at[n]) for n in range(4)]
    slab_copies = []
    for dx in range(4):
        for dl in range(2):
            there = ((x + dx) % 4) * 2 + (y + dl) % 2
            for second in range(2):
                at = pl.multiple_of((there + 8 * second) * BLK, BLK)
                slab_copies.append(
                    pltpu.make_async_copy(
                        slabs[dx * 2 + dl].at[pl.ds(second * BLK, BLK), :],
                        yraw.at[pl.ds(at, BLK), :],
                        slab_sem.at[(dx * 2 + dl) * 2 + second],
                    )
                )
    children = [
        pltpu.make_async_copy(front.at[2 * BLK :, BLK:], base, child_sem.at[0]),
        pltpu.make_async_copy(first, child.at[:, :, :, pl.ds(0, BLK)], child_sem.at[1]),
        pltpu.make_async_copy(rest, child.at[:, :, :, pl.ds(BLK, 3 * BLK)], child_sem.at[2]),
    ]
    start_all(slab_copies)
    raws[0].start()
    for k in range(3):
        start_all(factor_rows[k])
    for copy in slab_copies:
        copy.wait()
    panel_out[: 2 * BLK, :] = jnp.zeros((2 * BLK, BLK), F32)
    for k in range(PW // STEP):
        known = STEP * k
        if k % 2 == 0:
            raws[k // 2].wait()
            if k // 2 + 1 < len(raws):
                raws[k // 2 + 1].start()
        if k + 3 < blocks:
            start_all(factor_rows[k + 3])
        if k == 5:
            start_all(children)
        for copy in factor_rows[k]:
            copy.wait()
        strip = max(n for n, (start, _) in enumerate(STRIPS) if start <= known)
        wh, wl = inverses[2 * strip], inverses[2 * strip + 1]
        inner = k - STRIPS[strip][0] // STEP
        here = slice(known, known + STEP)
        value = yraw[here, :]
        if k:
            value = value - pairs(dot_nn, high[here, :known], low[here, :known], yh[:known, :], yl[:known, :])
        vh, vl = split(value)
        got = pairs(dot_nn, wh[inner], wl[inner], vh, vl)
        yh[here, :], yl[here, :] = split(got)

        def tile(t, carry, k=k, known=known, here=here, wh=wh, wl=wl, inner=inner):
            rows = pl.ds(pl.multiple_of(t * 512, 512), 512)
            value = jnp.concatenate([raw[2 * k, rows, :], raw[2 * k + 1, rows, :]], axis=1)
            if k:
                value = value - pairs(dot_nt, xh[rows, :known], xl[rows, :known], high[here, :known], low[here, :known])
            vh, vl = split(value)
            got = pairs(dot_nt, vh, vl, wh[inner], wl[inner])
            xh[rows, here], xl[rows, here] = split(got)
            for side in range(2):

                @pl.when(col == 2 * k + side)
                def _():
                    panel_out[pl.ds(pl.multiple_of(2 * BLK + t * 512, BLK), 512), :] = got[:, side * BLK : (side + 1) * BLK]

            return carry

        lax.fori_loop(0, raw.shape[1] // 512, tile, 0)
    lanes = pl.ds(pl.multiple_of(col * BLK, BLK), BLK)
    for second in range(2):
        block_row = row + 8 * second

        @pl.when(block_row >= col)
        def _():
            rows = pl.ds(pl.multiple_of(block_row * BLK, BLK), BLK)
            panel_out[second * BLK : (second + 1) * BLK, :] = high[rows, lanes].astype(F32) + low[rows, lanes].astype(F32)

    trailing[: 2 * BLK, :] = jnp.zeros((2 * BLK, trailing.shape[1]), F32)
    trailing[:, :BLK] = jnp.zeros((trailing.shape[0], BLK), F32)

    for copy in children:
        copy.wait()

    def assemble(q, carry):
        rows = pl.ds(pl.multiple_of(q * BLK, BLK), BLK)
        out = pl.ds(pl.multiple_of((q + 2) * BLK, BLK), BLK)
        for n in range(1, 5):
            total = base[rows, (n - 1) * BLK : n * BLK]
            for k in range(2):
                at = source[k, q + 2]
                use = at >= 0
                at = jnp.maximum(at, 0)
                for sel, j in ((1, n), (2, n - 1)):
                    if j < 4:
                        block = child[at, q & 1, :, j * BLK : (j + 1) * BLK]
                        total = total + jnp.where(use & (colsel[k, n] == sel), block, F32(0))
            trailing[out, n * BLK : (n + 1) * BLK] = total
        return carry

    lax.fori_loop(0, 8, assemble, 0)

    def update(t, carry):
        rows = pl.ds(pl.multiple_of(t * 512, 512), 512)
        out = pl.ds(pl.multiple_of(2 * BLK + t * 512, STEP), 512)
        trailing[out, BLK:] = trailing[out, BLK:] - pairs(dot_nn, xh[rows, :], xl[rows, :], yh[...], yl[...])
        return carry

    lax.fori_loop(0, raw.shape[1] // 512, update, 0)


def solve(place, source, colsel, strips, inverses, slabs, panel_rows, front, first, rest):
    rows, cols = front.shape
    under = rows - 2 * BLK
    return pl.pallas_call(
        solve_kernel,
        out_shape=[jax.ShapeDtypeStruct((rows, BLK), F32), jax.ShapeDtypeStruct((rows, cols), F32)],
        in_specs=[SMEM] * 3 + [ANY] * len(strips) + [VMEM] * len(inverses) + [ANY] * 12,
        out_specs=[VMEM, VMEM],
        scratch_shapes=[
            pltpu.VMEM((PW, PW), BF16),
            pltpu.VMEM((PW, PW), BF16),
            pltpu.VMEM((under, PW), BF16),
            pltpu.VMEM((under, PW), BF16),
            pltpu.VMEM((PW, cols - BLK), BF16),
            pltpu.VMEM((PW, cols - BLK), BF16),
            pltpu.VMEM((16, under, BLK), F32),
            pltpu.VMEM((PW, cols - BLK), F32),
            pltpu.VMEM((under, cols - BLK), F32),
            pltpu.VMEM((8, 2, BLK, 4 * BLK), F32),
            pltpu.SemaphoreType.DMA((PW // STEP, len(strips))),
            pltpu.SemaphoreType.DMA((4,)),
            pltpu.SemaphoreType.DMA((16,)),
            pltpu.SemaphoreType.DMA((3,)),
        ],
        compiler_params=PARAMS,
        name="solve",
    )(place, source, colsel, *strips, *inverses, *slabs, panel_rows, front, first, rest)


def local(front, updates, maps):
    row_at = lax.axis_index("row")
    col_at = lax.axis_index("col")
    place = jnp.stack([row_at // 2, (col_at // 8) * 2 + row_at % 2, (col_at // 2) % 4, col_at % 2]).astype(jnp.int32)
    slots = maps >> 4
    row_slots = lax.dynamic_index_in_dim(slots.reshape(2, 2, 8, 4), row_at, 2, keepdims=False)
    col_slots = lax.dynamic_index_in_dim(slots.reshape(2, 16, 4), col_at, 1, keepdims=False)

    slot = jnp.arange(5)
    own = jnp.pad(row_slots, ((0, 0), (0, 0), (0, 1)), constant_values=-1) == slot
    prior = jnp.pad(row_slots, ((0, 0), (0, 0), (1, 0)), constant_values=-1) == slot
    source = jnp.where(own, slot, jnp.where(prior, slot - 1, -8)) + 4 * jnp.arange(2)[:, None, None]
    source = source.transpose(0, 2, 1).reshape(2, 10).astype(jnp.int32)
    own = jnp.pad(col_slots, ((0, 0), (0, 1)), constant_values=-1) == slot
    prior = jnp.pad(col_slots, ((0, 0), (1, 0)), constant_values=-1) == slot
    colsel = jnp.where(own, 1, jnp.where(prior, 2, 0)).astype(jnp.int32)

    def outgoing(part):
        return part.reshape(2, 8, BLK, part.shape[1]).transpose(1, 0, 2, 3)

    def exchange(outgoing):
        return lax.all_to_all(outgoing, "row", split_axis=0, concat_axis=0, tiled=True)

    first = exchange(outgoing(updates[:, :BLK]))
    meets = col_slots[:, 0] == 0
    panel = front[:, :BLK].reshape(5, 2, BLK, BLK)
    parts = []
    for m in range(5):
        total = panel[m]
        for child in range(2):
            for a in (m, m - 1):
                if 0 <= a < 4:
                    hit = (row_slots[child, :, a] == m) & meets[child]
                    total = total + jnp.where(hit[:, None, None], first[4 * child + a], F32(0))
        parts.append(total)
    corner = parts[0].reshape(2 * BLK, BLK)
    under = jnp.stack(parts[1:]).reshape(8 * BLK, BLK)
    pieces, late = gather_leading(corner, place[1], place[3])

    tokens = [pieces[3][0, 0, 0, 0, 0]]
    panel_rows = lax.all_gather(held(under, tokens), "col", axis=0, tiled=True).reshape(16, 8 * BLK, BLK)
    late = around(held(late, tokens), 2)
    rest = exchange(held(outgoing(updates[:, BLK:]), tokens))

    strips, inverses = [], []

    def factor(call, place, pieces):
        got = factor_strip(call, place, pieces, strips)
        strips.extend(got[:2])
        inverses.extend(got[2:])

    factor(0, place, pieces)
    hit = (row_slots[:, :, 0] == 0).astype(jnp.int32)
    head, late = head_rows(hit, colsel, inverses[0], front, first, rest, late)
    late = [late, move(late, SWAP)]
    slabs = []
    for dx in range(4):
        for dl in range(2):
            if dx == 0 and dl == 0:
                slabs.append(head)
                continue
            there = [(r, ((r // 2 - dx) % 4) * 2 + (r + dl) % 2) for r in range(8)]
            slabs.append(lax.ppermute(head, "row", there))
    factor(1, place, late)
    factor(2, place, late)
    return tuple(solve(place, source, colsel, strips, inverses, slabs, panel_rows, front, first, rest))


def solution(mesh):
    in_specs = (P("row", "col"), P("row", "col"), P())
    out_specs = (P("row", "col"), P("row", "col"))
    return jax.shard_map(local, mesh=mesh, in_specs=in_specs, out_specs=out_specs, check_vma=False)
```

```python
import functools

import jax
import jax.numpy as jnp
from jax import lax
from jax.experimental import pallas as pl
from jax.experimental.pallas import tpu as pltpu
from jax.sharding import PartitionSpec as P

BLK = 128
PW = 2048
STRIPS = ((0, 1024), (1024, 512), (1536, 512))
SLABS = (0, 1, 3, 2)
ROWS = 512
STEP = 256
BOTH = ("row", "col")
OFFSETS = (0, -1, 1, 2)
NEAR = 2
F32 = jnp.float32
BF16 = jnp.bfloat16
PARAMS = pltpu.CompilerParams(vmem_limit_bytes=58 << 20)
ANY = pl.BlockSpec(memory_space=pl.ANY)
VMEM = pl.BlockSpec(memory_space=pltpu.VMEM)
SMEM = pl.BlockSpec(memory_space=pltpu.SMEM)


def flat(x, y, z, core):
    return ((x % 4) * 2 + y % 2) * 16 + ((y % 4) // 2) * 8 + (z % 4) * 2 + core % 2


def move(value, *by):
    every = [(x, y, z, c) for x in range(4) for y in range(4) for z in range(4) for c in range(2)]
    pairs = []
    for x, y, z, c in every:
        step = by[c] if len(by) > 1 else by[0]
        if step is not None:
            pairs.append((flat(x, y, z, c), flat(x + step[0], y + step[1], z + step[2], c + step[3])))
    return lax.ppermute(value, BOTH, pairs)


SWAP = (0, 0, 0, 1)


def around(value, *axes):
    out = [value]
    for offset in OFFSETS[1:]:
        out.append(move(value, *[tuple(-offset if n == axis else 0 for n in range(4)) for axis in axes]))
    return out


def held(array, tokens):
    array = lax.optimization_barrier(array)
    ready = functools.reduce(jnp.logical_and, [token <= F32(jnp.finfo(jnp.float32).max) for token in tokens])
    at = (0,) * array.ndim
    first = jnp.where(ready, array[at], F32(0)).reshape((1,) * array.ndim)
    return lax.dynamic_update_slice(array, first, at)


def gather_leading(corner, y_at, core_at):
    first = core_at == 0
    upper, lower = corner[:BLK], corner[BLK:]
    mine = jnp.where(first, upper, lower)
    other = move(jnp.where(first, lower, upper), SWAP)
    both = jnp.stack([jnp.where(first, mine, other), jnp.where(first, other, mine)])
    own, below, above, opposite = around(both, 1)
    blocks = []
    for y in range(4):
        d = (y - y_at) & 3
        blocks.append(jnp.where(d == 0, own, jnp.where(d == 1, above, jnp.where(d == 2, opposite, below))))
    group = jnp.stack(around(jnp.stack(blocks), 2, 0))
    mine = around(group[:, :2], 0, 2)
    pieces = [*mine, *[move(piece, SWAP) for piece in mine]]
    late = jnp.where(first, move(group[:, 2], SWAP), group[:, 3])
    return pieces, late


def eliminate(tiles):
    tiles = list(tiles)
    count = len(tiles)
    lane = lax.broadcasted_iota(jnp.int32, (8, BLK), 1)
    sub = lax.broadcasted_iota(jnp.int32, (8, BLK), 0)
    upper = []

    def by_lane(x, j):
        return jnp.broadcast_to(x[:, j : j + 1], (8, BLK))

    def by_sub(x, s):
        return jnp.broadcast_to(x[s : s + 1, :], (8, BLK))

    for p in range(count):
        now = tiles[p]
        o = 8 * p
        inside = (lane >= o) & (lane < o + 8)
        column = [by_lane(now, o + t) for t in range(8)]
        a = {(s, t): by_sub(column[t], s) for t in range(8) for s in range(t, 8)}
        rows = [by_sub(now, t) for t in range(8)]
        unit = [jnp.where(lane == o + t, F32(1), jnp.where(inside, F32(0), rows[t])) for t in range(8)]
        r = []
        low = {}
        for t in range(8):
            r.append(lax.rsqrt(a[t, t]))
            for s in range(t + 1, 8):
                low[s, t] = a[s, t] * r[t]
            for u in range(t + 1, 8):
                for s in range(u, 8):
                    a[s, u] = a[s, u] - low[s, t] * low[u, t]
        z = []
        q = []
        for t in range(8):
            z_now, q_now = unit[t], rows[t]
            for s in range(t):
                z_now = z_now - low[t, s] * z[s]
                q_now = q_now - low[t, s] * q[s]
            z.append(z_now * r[t])
            q.append(q_now * r[t])
        y = [None] * 8
        for t in reversed(range(8)):
            y_now = z[t]
            for s in range(t + 1, 8):
                y_now = y_now - low[s, t] * y[s]
            y[t] = y_now * r[t]
        z_tile, q_tile, y_tile = z[0], q[0], y[0]
        for t in range(1, 8):
            z_tile = jnp.where(sub == t, z[t], z_tile)
            q_tile = jnp.where(sub == t, q[t], q_tile)
            y_tile = jnp.where(sub == t, y[t], y_tile)
        upper.append(jnp.where(lane >= o + sub, q_tile, F32(0)))
        tiles[p] = jnp.where(lane <= o + sub, z_tile, F32(0))
        for i in range(p + 1, min(p + 1 + NEAR, count)):
            terms = [by_lane(tiles[i], o + t) * y[t] for t in range(8)]
            while len(terms) > 1:
                terms = [terms[k] + terms[k + 1] for k in range(0, len(terms), 2)]
            tiles[i] = jnp.where(inside, F32(0), tiles[i]) - terms[0]
        far = p + 1 + NEAR
        if far < count:
            zero = jnp.zeros((8, BLK), F32)
            padded = jnp.concatenate([zero] * p + [y_tile] + [zero] * (count - p - 1), axis=0)
            less = exact_nn(jnp.concatenate(tiles[far:], axis=0), padded)
            for i in range(far, count):
                tiles[i] = jnp.where(inside, F32(0), tiles[i]) - less[8 * (i - far) : 8 * (i - far) + 8]
    return tiles, upper


def split(x):
    high = x.astype(BF16)
    return high, (x - high.astype(F32)).astype(BF16)


def dot_nt(a, b):
    return lax.dot_general(a, b, (((1,), (1,)), ((), ())), preferred_element_type=F32)


def dot_nn(a, b):
    return lax.dot_general(a, b, (((1,), (0,)), ((), ())), preferred_element_type=F32)


def pairs(dot, ah, al, bh, bl):
    return dot(ah, bh) + (dot(ah, bl) + dot(al, bh))


def exact_nt(a, b):
    return lax.dot_general(a, b, (((1,), (1,)), ((), ())), precision=lax.Precision.HIGHEST, preferred_element_type=F32)


def near_nt(a, b):
    return pairs(dot_nt, *split(a), *split(b))


def near_nn(a, b):
    return pairs(dot_nn, *split(a), *split(b))


def exact_nn(a, b):
    return jnp.dot(a, b, precision=lax.Precision.HIGHEST, preferred_element_type=F32)


def offset_of(index):
    return jnp.where(index == 3, 2, jnp.where(index == 2, 1, jnp.where(index == 1, -1, 0)))


def load_leading(place, pieces, late, dest, sems, first_col):
    x, z, core = place[0], place[2], place[3]
    count = dest.shape[0]

    def fetch(source, block_row, block_col):
        pltpu.make_async_copy(
            source,
            dest.at[block_col, pl.ds(pl.multiple_of(block_row * BLK, BLK), BLK), :],
            sems.at[block_col >> 2],
        ).start()

    if late:
        for swapped, ref in enumerate(pieces):
            low_y = (core + swapped) & 1

            def one(n, carry, ref=ref, low_y=low_y):
                far, near, c = n >> 3, (n >> 1) & 3, n & 1
                block_row = ((x + offset_of(near)) & 3) * 2 + low_y + 8
                block_col = 8 + ((z + offset_of(far)) & 3) * 2 + c - first_col

                @pl.when((block_col >= 0) & (block_col < count))
                def _():
                    fetch(ref.at[far, near, c], block_row, block_col)

                return carry

            lax.fori_loop(0, 32, one, 0)
        return
    for number, ref in enumerate(pieces):
        half = (core + number // 4) & 1
        far = OFFSETS[number % 4]

        def one(n, carry, ref=ref, half=half, far=far):
            i, y, c = n >> 2, (n >> 1) & 1, n & 1
            near = offset_of(i)
            dx, dz = jnp.where(half == 0, far, near), jnp.where(half == 0, near, far)
            fetch(ref.at[i, y, c], ((x + dx) & 3) * 2 + y + 8 * half, ((z + dz) & 3) * 2 + c - first_col)
            return carry

        lax.fori_loop(0, 16, one, 0)


def factor_kernel(call, place, *refs):
    start, width = STRIPS[call]
    late = start >= PW // 2
    count = 2 if late else 8
    pieces, refs = refs[:count], refs[count:]
    earlier = refs[: 2 * call]
    out_high, out_low, inv_high, inv_low = refs[2 * call : 4 + 2 * call]
    (lead, high, low, c, diag, inverse, upper, inverse1, low21, load_sem, strip_sem, out_sem) = refs[4 + 2 * call :]
    load_leading(place, pieces, late, lead, load_sem, start // BLK)
    copies = []
    for n in range(call):
        for which, dest in ((0, high), (1, low)):
            copies.append(
                pltpu.make_async_copy(
                    earlier[2 * n + which].at[pl.ds(start - STRIPS[n][0], PW - start), :],
                    dest.at[:, pl.ds(*STRIPS[n])],
                    strip_sem.at[2 * n + which],
                )
            )
    for copy in copies:
        copy.start()

    def wait_lead(n):
        loaded = lead.at[4 * n : 4 * n + 4, PW // 2 if late else 0 :, :]
        pltpu.make_async_copy(loaded, loaded, load_sem.at[n]).wait()

    def outs(kk):
        rows, cols = pl.ds(STEP * kk, PW - start - STEP * kk), pl.ds(STEP * kk, STEP)
        source = pl.ds(start + STEP * kk, STEP)
        return [
            pltpu.make_async_copy(high.at[rows, source], out_high.at[rows, cols], out_sem.at[2 * kk]),
            pltpu.make_async_copy(low.at[rows, source], out_low.at[rows, cols], out_sem.at[2 * kk + 1]),
        ]

    wait_lead(0)
    for copy in copies:
        copy.wait()

    def put(rows, cols, value):
        h, l = split(value)
        high[rows, cols] = h
        low[rows, cols] = l

    def under(at, tile):
        wide = (PW - start - at) // 512

        def one(t, carry):
            tile(pl.multiple_of(at + t * 512, STEP), 512)
            return carry

        lax.fori_loop(0, wide, one, 0)
        if at + wide * 512 < PW - start:
            tile(at + wide * 512, STEP)

    def before(kk):
        if kk and kk % 2 == 0:
            wait_lead(kk // 2)
        known = start + STEP * kk
        r0 = STEP * kk

        def tile(at, size):
            rows = pl.ds(at, size)
            whole = pl.ds(pl.multiple_of(start + at, STEP), size)
            value = jnp.concatenate([lead[2 * kk, whole, :], lead[2 * kk + 1, whole, :]], axis=1)
            if known > 0:
                value = value - pairs(
                    dot_nt, high[rows, :known], low[rows, :known], high[r0 : r0 + STEP, :known], low[r0 : r0 + STEP, :known]
                )
            c[rows, :] = value

        tile(r0, STEP)
        under(r0 + STEP, tile)
        diag[...] = c[r0 : r0 + BLK, :BLK]

    def between(kk):
        r0 = STEP * kk
        col = start + r0
        w1 = inverse[...]
        l21 = near_nt(c[r0 + BLK : r0 + STEP, :BLK], w1)
        diag[...] = c[r0 + BLK : r0 + STEP, BLK:] - near_nt(l21, l21)
        inverse1[...] = w1
        low21[...] = l21
        put(pl.ds(r0, BLK), pl.ds(col, BLK), upper[...].T)
        put(pl.ds(r0, BLK), pl.ds(col + BLK, BLK), jnp.zeros((BLK, BLK), F32))
        put(pl.ds(r0 + BLK, BLK), pl.ds(col, BLK), l21)

    def after(kk):
        r0 = STEP * kk
        col = start + r0
        w2 = inverse[...]
        put(pl.ds(r0 + BLK, BLK), pl.ds(col + BLK, BLK), upper[...].T)
        w21 = -near_nn(w2, near_nn(low21[...], inverse1[...]))
        top = jnp.concatenate([inverse1[...], jnp.zeros((BLK, BLK), F32)], axis=1)
        w = jnp.concatenate([top, jnp.concatenate([w21, w2], axis=1)], axis=0)
        wh, wl = split(w)
        inv_high[kk] = wh
        inv_low[kk] = wl

        def tile(at, size):
            rows = pl.ds(at, size)
            ch, cl = split(c[rows, :])
            put(rows, pl.ds(col, STEP), pairs(dot_nt, ch, cl, inv_high[kk], inv_low[kk]))

        under(r0 + STEP, tile)
        for copy in outs(kk):
            copy.start()

    def half(h, carry):
        for kk in range(width // STEP):
            pl.when(h == 2 * kk)(functools.partial(before, kk))
        w, u = eliminate([diag[8 * i : 8 * i + 8, :] for i in range(16)])
        for i in range(16):
            inverse[8 * i : 8 * i + 8, :] = w[i]
            upper[8 * i : 8 * i + 8, :] = u[i]
        for kk in range(width // STEP):
            pl.when(h == 2 * kk)(functools.partial(between, kk))
            pl.when(h == 2 * kk + 1)(functools.partial(after, kk))
        return carry

    lax.fori_loop(0, width // BLK, half, 0)
    for kk in range(width // STEP):
        for copy in outs(kk):
            copy.wait()


def factor_strip(call, place, pieces, earlier):
    start, width = STRIPS[call]
    rows = PW - start
    known = start + width
    strip = jax.ShapeDtypeStruct((rows, width), BF16)
    inverses = jax.ShapeDtypeStruct((width // STEP, STEP, STEP), BF16)
    block = pltpu.VMEM((BLK, BLK), F32)
    return pl.pallas_call(
        functools.partial(factor_kernel, call),
        out_shape=[strip, strip, inverses, inverses],
        in_specs=[SMEM] + [ANY] * (len(pieces) + 2 * call),
        out_specs=[ANY, ANY, VMEM, VMEM],
        scratch_shapes=[
            pltpu.VMEM((width // BLK, PW, BLK), F32),
            pltpu.VMEM((rows, known), BF16),
            pltpu.VMEM((rows, known), BF16),
            pltpu.VMEM((rows, STEP), F32),
            block,
            block,
            block,
            block,
            block,
            pltpu.SemaphoreType.DMA((width // 512,)),
            pltpu.SemaphoreType.DMA((max(2 * call, 1),)),
            pltpu.SemaphoreType.DMA((2 * width // STEP,)),
        ],
        compiler_params=PARAMS,
        cost_estimate=pl.CostEstimate(flops=int(7e7) * width, bytes_accessed=int(1e8), transcendentals=0),
        name=f"factor{call}",
    )(place, *pieces, *earlier)


def head_kernel(hit, colsel, token, front, f0, f1, g0, g1, own, below, above, opposite, head, late):
    del token
    for n, ref in enumerate((own, below, above, opposite)):
        late[n] = ref[...]
    for w in range(2):
        rows = slice(w * BLK, (w + 1) * BLK)
        for n in range(1, 5):
            total = front[rows, n * BLK : (n + 1) * BLK]
            for k, (first, rest) in enumerate(((f0, g0), (f1, g1))):
                for sel, j in ((1, n), (2, n - 1)):
                    if j < 4:
                        block = first[0, w] if j == 0 else rest[0, w, :, (j - 1) * BLK : j * BLK]
                        use = (hit[k, w] == 1) & (colsel[k, n] == sel)
                        total = total + jnp.where(use, block, F32(0))
            head[rows, (n - 1) * BLK : n * BLK] = total


def head_rows(hit, colsel, token, front, first, rest, late):
    cols = front.shape[1]

    def child(k):
        return lambda i: (4 * k, 0, 0, 0)

    return pl.pallas_call(
        head_kernel,
        grid=(1,),
        out_shape=[
            jax.ShapeDtypeStruct((2 * BLK, cols - BLK), F32),
            jax.ShapeDtypeStruct((4, *late[0].shape), F32),
        ],
        in_specs=[
            SMEM,
            SMEM,
            ANY,
            pl.BlockSpec((2 * BLK, cols), lambda i: (0, 0)),
            pl.BlockSpec((1, 2, BLK, BLK), child(0)),
            pl.BlockSpec((1, 2, BLK, BLK), child(1)),
            pl.BlockSpec((1, 2, BLK, 3 * BLK), child(0)),
            pl.BlockSpec((1, 2, BLK, 3 * BLK), child(1)),
            VMEM,
            VMEM,
            VMEM,
            VMEM,
        ],
        out_specs=[pl.BlockSpec((2 * BLK, cols - BLK), lambda i: (0, 0)), VMEM],
        compiler_params=PARAMS,
        name="head",
    )(hit, colsel, token, front, first, first, rest, rest, *late)


def solve_kernel(place, source, colsel, *refs):
    n_strips = 2 * len(STRIPS)
    strips, inverses, refs = refs[:n_strips], refs[n_strips : 2 * n_strips], refs[2 * n_strips :]
    slabs, refs = refs[:8], refs[8:]
    panel_rows, front, first, rest, panel_out, trailing = refs[:6]
    high, low, xh, xl, yh, yl, raw, yraw, base, child, sems, raw_sem, slab_sem, child_sem = refs[6:]
    x, y, z, core = place[0], place[1], place[2], place[3]
    row = x * 2 + y % 2
    col = (y // 2) * 8 + z * 2 + core
    blocks = PW // STEP
    factor_rows = [[] for _ in range(blocks)]
    for k in range(blocks):
        for n, (start, width) in enumerate(STRIPS):
            if start <= STEP * k:
                cols = min(width, STEP * (k + 1) - start)
                for which, dest in ((0, high), (1, low)):
                    factor_rows[k].append(
                        pltpu.make_async_copy(
                            strips[2 * n + which].at[pl.ds(STEP * k - start, STEP), pl.ds(0, cols)],
                            dest.at[pl.ds(STEP * k, STEP), pl.ds(start, cols)],
                            sems.at[k, 2 * n + which],
                        )
                    )

    def start_all(copies):
        for copy in copies:
            copy.start()

    raws = [pltpu.make_async_copy(panel_rows.at[pl.ds(4 * n, 4)], raw.at[pl.ds(4 * n, 4)], raw_sem.at[n]) for n in range(4)]
    slab_copies = []
    for n, dx in enumerate(SLABS):
        for dl in range(2):
            there = ((x + dx) % 4) * 2 + (y + dl) % 2
            for second in range(2):
                at = pl.multiple_of((there + 8 * second) * BLK, BLK)
                slab_copies.append(
                    pltpu.make_async_copy(
                        slabs[n * 2 + dl].at[pl.ds(second * BLK, BLK), :],
                        yraw.at[pl.ds(at, BLK), :],
                        slab_sem.at[(n * 2 + dl) * 2 + second],
                    )
                )
    children = [
        pltpu.make_async_copy(front.at[2 * BLK :, BLK:], base, child_sem.at[0]),
        pltpu.make_async_copy(first, child.at[:, :, :, pl.ds(0, BLK)], child_sem.at[1]),
        pltpu.make_async_copy(rest, child.at[:, :, :, pl.ds(BLK, 3 * BLK)], child_sem.at[2]),
    ]
    start_all(slab_copies)
    raws[0].start()
    for k in range(3):
        start_all(factor_rows[k])
    for copy in slab_copies:
        copy.wait()
    panel_out[: 2 * BLK, :] = jnp.zeros((2 * BLK, BLK), F32)
    for k in range(PW // STEP):
        known = STEP * k
        if k % 2 == 0:
            raws[k // 2].wait()
            if k // 2 + 1 < len(raws):
                raws[k // 2 + 1].start()
        if k + 3 < blocks:
            start_all(factor_rows[k + 3])
        if k == 5:
            start_all(children)
        for copy in factor_rows[k]:
            copy.wait()
        strip = max(n for n, (start, _) in enumerate(STRIPS) if start <= known)
        wh, wl = inverses[2 * strip], inverses[2 * strip + 1]
        inner = k - STRIPS[strip][0] // STEP
        here = slice(known, known + STEP)
        value = yraw[here, :]
        if k:
            value = value - pairs(dot_nn, high[here, :known], low[here, :known], yh[:known, :], yl[:known, :])
        vh, vl = split(value)
        got = pairs(dot_nn, wh[inner], wl[inner], vh, vl)
        yh[here, :], yl[here, :] = split(got)

        if k % 2 == 0:
            first_inverse = wh[inner], wl[inner]
            continue
        done = known - STEP
        two = slice(done, done + 2 * STEP)
        front_half, back_half = slice(done, known), here

        def tile(t, carry, k=k, done=done, two=two, a=front_half, b=back_half, wa=first_inverse, wb=(wh[inner], wl[inner])):
            rows = pl.ds(pl.multiple_of(t * ROWS, ROWS), ROWS)
            value = jnp.concatenate([raw[2 * k - 2 + n, rows, :] for n in range(4)], axis=1)
            if done:
                value = value - pairs(dot_nt, xh[rows, :done], xl[rows, :done], high[two, :done], low[two, :done])
            xa = pairs(dot_nt, *split(value[:, :STEP]), *wa)
            xah, xal = split(xa)
            vb = value[:, STEP:] - pairs(dot_nt, xah, xal, high[b, a], low[b, a])
            xb = pairs(dot_nt, *split(vb), *wb)
            xh[rows, a], xl[rows, a] = xah, xal
            xh[rows, b], xl[rows, b] = split(xb)
            for side in range(4):

                @pl.when(col == 2 * k - 2 + side)
                def _():
                    got = (xa, xb)[side // 2]
                    at = pl.multiple_of(2 * BLK + t * ROWS, BLK)
                    panel_out[pl.ds(at, ROWS), :] = got[:, (side % 2) * BLK : (side % 2 + 1) * BLK]

            return carry

        lax.fori_loop(0, raw.shape[1] // ROWS, tile, 0)
    lanes = pl.ds(pl.multiple_of(col * BLK, BLK), BLK)
    for second in range(2):
        block_row = row + 8 * second

        @pl.when(block_row >= col)
        def _():
            rows = pl.ds(pl.multiple_of(block_row * BLK, BLK), BLK)
            panel_out[second * BLK : (second + 1) * BLK, :] = high[rows, lanes].astype(F32) + low[rows, lanes].astype(F32)

    trailing[: 2 * BLK, :] = jnp.zeros((2 * BLK, trailing.shape[1]), F32)
    trailing[:, :BLK] = jnp.zeros((trailing.shape[0], BLK), F32)

    for copy in children:
        copy.wait()

    def assemble(q, carry):
        rows = pl.ds(pl.multiple_of(q * BLK, BLK), BLK)
        out = pl.ds(pl.multiple_of((q + 2) * BLK, BLK), BLK)
        for n in range(1, 5):
            total = base[rows, (n - 1) * BLK : n * BLK]
            for k in range(2):
                at = source[k, q + 2]
                use = at >= 0
                at = jnp.maximum(at, 0)
                for sel, j in ((1, n), (2, n - 1)):
                    if j < 4:
                        block = child[at, q & 1, :, j * BLK : (j + 1) * BLK]
                        total = total + jnp.where(use & (colsel[k, n] == sel), block, F32(0))
            trailing[out, n * BLK : (n + 1) * BLK] = total
        return carry

    lax.fori_loop(0, 8, assemble, 0)

    def update(t, carry):
        rows = pl.ds(pl.multiple_of(t * 512, 512), 512)
        out = pl.ds(pl.multiple_of(2 * BLK + t * 512, STEP), 512)
        trailing[out, BLK:] = trailing[out, BLK:] - pairs(dot_nn, xh[rows, :], xl[rows, :], yh[...], yl[...])
        return carry

    lax.fori_loop(0, raw.shape[1] // 512, update, 0)


def solve(place, source, colsel, strips, inverses, slabs, panel_rows, front, first, rest):
    rows, cols = front.shape
    under = rows - 2 * BLK
    return pl.pallas_call(
        solve_kernel,
        out_shape=[jax.ShapeDtypeStruct((rows, BLK), F32), jax.ShapeDtypeStruct((rows, cols), F32)],
        in_specs=[SMEM] * 3 + [ANY] * len(strips) + [VMEM] * len(inverses) + [ANY] * 12,
        out_specs=[VMEM, VMEM],
        scratch_shapes=[
            pltpu.VMEM((PW, PW), BF16),
            pltpu.VMEM((PW, PW), BF16),
            pltpu.VMEM((under, PW), BF16),
            pltpu.VMEM((under, PW), BF16),
            pltpu.VMEM((PW, cols - BLK), BF16),
            pltpu.VMEM((PW, cols - BLK), BF16),
            pltpu.VMEM((16, under, BLK), F32),
            pltpu.VMEM((PW, cols - BLK), F32),
            pltpu.VMEM((under, cols - BLK), F32),
            pltpu.VMEM((8, 2, BLK, 4 * BLK), F32),
            pltpu.SemaphoreType.DMA((PW // STEP, len(strips))),
            pltpu.SemaphoreType.DMA((4,)),
            pltpu.SemaphoreType.DMA((16,)),
            pltpu.SemaphoreType.DMA((3,)),
        ],
        compiler_params=PARAMS,
        name="solve",
    )(place, source, colsel, *strips, *inverses, *slabs, panel_rows, front, first, rest)


def local(front, updates, maps):
    row_at = lax.axis_index("row")
    col_at = lax.axis_index("col")
    place = jnp.stack([row_at // 2, (col_at // 8) * 2 + row_at % 2, (col_at // 2) % 4, col_at % 2]).astype(jnp.int32)
    slots = maps >> 4
    row_slots = lax.dynamic_index_in_dim(slots.reshape(2, 2, 8, 4), row_at, 2, keepdims=False)
    col_slots = lax.dynamic_index_in_dim(slots.reshape(2, 16, 4), col_at, 1, keepdims=False)

    slot = jnp.arange(5)
    own = jnp.pad(row_slots, ((0, 0), (0, 0), (0, 1)), constant_values=-1) == slot
    prior = jnp.pad(row_slots, ((0, 0), (0, 0), (1, 0)), constant_values=-1) == slot
    source = jnp.where(own, slot, jnp.where(prior, slot - 1, -8)) + 4 * jnp.arange(2)[:, None, None]
    source = source.transpose(0, 2, 1).reshape(2, 10).astype(jnp.int32)
    own = jnp.pad(col_slots, ((0, 0), (0, 1)), constant_values=-1) == slot
    prior = jnp.pad(col_slots, ((0, 0), (1, 0)), constant_values=-1) == slot
    colsel = jnp.where(own, 1, jnp.where(prior, 2, 0)).astype(jnp.int32)

    def outgoing(part):
        return part.reshape(2, 8, BLK, part.shape[1]).transpose(1, 0, 2, 3)

    def exchange(outgoing):
        return lax.all_to_all(outgoing, "row", split_axis=0, concat_axis=0, tiled=True)

    first = exchange(outgoing(updates[:, :BLK]))
    meets = col_slots[:, 0] == 0
    panel = front[:, :BLK].reshape(5, 2, BLK, BLK)
    parts = []
    for m in range(5):
        total = panel[m]
        for child in range(2):
            for a in (m, m - 1):
                if 0 <= a < 4:
                    hit = (row_slots[child, :, a] == m) & meets[child]
                    total = total + jnp.where(hit[:, None, None], first[4 * child + a], F32(0))
        parts.append(total)
    whole = lax.optimization_barrier(jnp.stack(parts).reshape(10 * BLK, BLK))
    corner = whole[: 2 * BLK]
    under = whole[2 * BLK :]
    pieces, late = gather_leading(corner, place[1], place[3])

    tokens = [pieces[3][0, 0, 0, 0, 0]]
    panel_rows = lax.all_gather(held(under, tokens), "col", axis=0, tiled=True).reshape(16, 8 * BLK, BLK)
    late = around(held(late, tokens), 2)
    rest = exchange(held(outgoing(updates[:, BLK:]), tokens))

    strips, inverses = [], []

    def factor(call, place, pieces):
        got = factor_strip(call, place, pieces, strips)
        strips.extend(got[:2])
        inverses.extend(got[2:])

    factor(0, place, pieces)
    hit = (row_slots[:, :, 0] == 0).astype(jnp.int32)
    head, late = head_rows(hit, colsel, inverses[0], front, first, rest, late)
    late = [late, move(late, SWAP)]
    slabs = []
    for dx in SLABS:
        for dl in range(2):
            there = [(r, ((r // 2 - dx) % 4) * 2 + (r + dl) % 2) for r in range(8)]
            slabs.append(lax.ppermute(head, "row", there) if dx or dl else head)
    factor(1, place, late)
    factor(2, place, late)
    return tuple(solve(place, source, colsel, strips, inverses, slabs, panel_rows, front, first, rest))


def solution(mesh):
    in_specs = (P("row", "col"), P("row", "col"), P())
    out_specs = (P("row", "col"), P("row", "col"))
    return jax.shard_map(local, mesh=mesh, in_specs=in_specs, out_specs=out_specs, check_vma=False)
```

```python
import functools

import jax
import jax.numpy as jnp
from jax import lax
from jax.experimental import pallas as pl
from jax.experimental.pallas import tpu as pltpu
from jax.sharding import PartitionSpec as P

BLK = 128
PW = 2048
STRIPS = ((0, 1024), (1024, 512), (1536, 512))
SLABS = (0, 1, 3, 2)
ROWS = 512
STEP = 256
BOTH = ("row", "col")
OFFSETS = (0, -1, 1, 2)
NEAR = 2
F32 = jnp.float32
BF16 = jnp.bfloat16
PARAMS = pltpu.CompilerParams(vmem_limit_bytes=58 << 20)
ANY = pl.BlockSpec(memory_space=pl.ANY)
VMEM = pl.BlockSpec(memory_space=pltpu.VMEM)
SMEM = pl.BlockSpec(memory_space=pltpu.SMEM)


def flat(x, y, z, core):
    return ((x % 4) * 2 + y % 2) * 16 + ((y % 4) // 2) * 8 + (z % 4) * 2 + core % 2


def move(value, *by):
    every = [(x, y, z, c) for x in range(4) for y in range(4) for z in range(4) for c in range(2)]
    pairs = []
    for x, y, z, c in every:
        step = by[c] if len(by) > 1 else by[0]
        if step is not None:
            pairs.append((flat(x, y, z, c), flat(x + step[0], y + step[1], z + step[2], c + step[3])))
    return lax.ppermute(value, BOTH, pairs)


SWAP = (0, 0, 0, 1)


def around(value, *axes):
    out = [value]
    for offset in OFFSETS[1:]:
        out.append(move(value, *[tuple(-offset if n == axis else 0 for n in range(4)) for axis in axes]))
    return out


def held(array, tokens):
    array = lax.optimization_barrier(array)
    ready = functools.reduce(jnp.logical_and, [token <= F32(jnp.finfo(jnp.float32).max) for token in tokens])
    at = (0,) * array.ndim
    first = jnp.where(ready, array[at], F32(0)).reshape((1,) * array.ndim)
    return lax.dynamic_update_slice(array, first, at)


def gather_leading(corner, y_at, core_at):
    first = core_at == 0
    upper, lower = corner[:BLK], corner[BLK:]
    mine = jnp.where(first, upper, lower)
    other = move(jnp.where(first, lower, upper), SWAP)
    both = jnp.stack([jnp.where(first, mine, other), jnp.where(first, other, mine)])
    own, below, above, opposite = around(both, 1)
    blocks = []
    for y in range(4):
        d = (y - y_at) & 3
        blocks.append(jnp.where(d == 0, own, jnp.where(d == 1, above, jnp.where(d == 2, opposite, below))))
    group = jnp.stack(around(jnp.stack(blocks), 2, 0))
    mine = around(group[:, :2], 0, 2)
    pieces = [*mine, *[move(piece, SWAP) for piece in mine]]
    late = jnp.where(first, move(group[:, 2], SWAP), group[:, 3])
    return pieces, late


def eliminate(tiles):
    tiles = list(tiles)
    count = len(tiles)
    lane = lax.broadcasted_iota(jnp.int32, (8, BLK), 1)
    sub = lax.broadcasted_iota(jnp.int32, (8, BLK), 0)
    upper = []

    def by_lane(x, j):
        return jnp.broadcast_to(x[:, j : j + 1], (8, BLK))

    def by_sub(x, s):
        return jnp.broadcast_to(x[s : s + 1, :], (8, BLK))

    for p in range(count):
        now = tiles[p]
        o = 8 * p
        inside = (lane >= o) & (lane < o + 8)
        column = [by_lane(now, o + t) for t in range(8)]
        a = {(s, t): by_sub(column[t], s) for t in range(8) for s in range(t, 8)}
        rows = [by_sub(now, t) for t in range(8)]
        unit = [jnp.where(lane == o + t, F32(1), jnp.where(inside, F32(0), rows[t])) for t in range(8)]
        r = []
        low = {}
        for t in range(8):
            r.append(lax.rsqrt(a[t, t]))
            for s in range(t + 1, 8):
                low[s, t] = a[s, t] * r[t]
            for u in range(t + 1, 8):
                for s in range(u, 8):
                    a[s, u] = a[s, u] - low[s, t] * low[u, t]
        z = []
        q = []
        for t in range(8):
            z_now, q_now = unit[t], rows[t]
            for s in range(t):
                z_now = z_now - low[t, s] * z[s]
                q_now = q_now - low[t, s] * q[s]
            z.append(z_now * r[t])
            q.append(q_now * r[t])
        y = [None] * 8
        for t in reversed(range(8)):
            y_now = z[t]
            for s in range(t + 1, 8):
                y_now = y_now - low[s, t] * y[s]
            y[t] = y_now * r[t]
        z_tile, q_tile, y_tile = z[0], q[0], y[0]
        for t in range(1, 8):
            z_tile = jnp.where(sub == t, z[t], z_tile)
            q_tile = jnp.where(sub == t, q[t], q_tile)
            y_tile = jnp.where(sub == t, y[t], y_tile)
        upper.append(jnp.where(lane >= o + sub, q_tile, F32(0)))
        tiles[p] = jnp.where(lane <= o + sub, z_tile, F32(0))
        for i in range(p + 1, min(p + 1 + NEAR, count)):
            terms = [by_lane(tiles[i], o + t) * y[t] for t in range(8)]
            while len(terms) > 1:
                terms = [terms[k] + terms[k + 1] for k in range(0, len(terms), 2)]
            tiles[i] = jnp.where(inside, F32(0), tiles[i]) - terms[0]
        far = p + 1 + NEAR
        if far < count:
            zero = jnp.zeros((8, BLK), F32)
            padded = jnp.concatenate([zero] * p + [y_tile] + [zero] * (count - p - 1), axis=0)
            less = exact_nn(jnp.concatenate(tiles[far:], axis=0), padded)
            for i in range(far, count):
                tiles[i] = jnp.where(inside, F32(0), tiles[i]) - less[8 * (i - far) : 8 * (i - far) + 8]
    return tiles, upper


def split(x):
    high = x.astype(BF16)
    return high, (x - high.astype(F32)).astype(BF16)


def dot_nt(a, b):
    return lax.dot_general(a, b, (((1,), (1,)), ((), ())), preferred_element_type=F32)


def dot_nn(a, b):
    return lax.dot_general(a, b, (((1,), (0,)), ((), ())), preferred_element_type=F32)


def pairs(dot, ah, al, bh, bl):
    return dot(ah, bh) + (dot(ah, bl) + dot(al, bh))


def exact_nt(a, b):
    return lax.dot_general(a, b, (((1,), (1,)), ((), ())), precision=lax.Precision.HIGHEST, preferred_element_type=F32)


def near_nt(a, b):
    return pairs(dot_nt, *split(a), *split(b))


def near_nn(a, b):
    return pairs(dot_nn, *split(a), *split(b))


def exact_nn(a, b):
    return jnp.dot(a, b, precision=lax.Precision.HIGHEST, preferred_element_type=F32)


def offset_of(index):
    return jnp.where(index == 3, 2, jnp.where(index == 2, 1, jnp.where(index == 1, -1, 0)))


def load_leading(place, pieces, late, dest, sems, first_col):
    x, z, core = place[0], place[2], place[3]
    count = dest.shape[0]

    def fetch(source, block_row, block_col):
        pltpu.make_async_copy(
            source,
            dest.at[block_col, pl.ds(pl.multiple_of(block_row * BLK, BLK), BLK), :],
            sems.at[block_col >> 2],
        ).start()

    if late:
        for swapped, ref in enumerate(pieces):
            low_y = (core + swapped) & 1

            def one(n, carry, ref=ref, low_y=low_y):
                far, near, c = n >> 3, (n >> 1) & 3, n & 1
                block_row = ((x + offset_of(near)) & 3) * 2 + low_y + 8
                block_col = 8 + ((z + offset_of(far)) & 3) * 2 + c - first_col

                @pl.when((block_col >= 0) & (block_col < count))
                def _():
                    fetch(ref.at[far, near, c], block_row, block_col)

                return carry

            lax.fori_loop(0, 32, one, 0)
        return
    for number, ref in enumerate(pieces):
        half = (core + number // 4) & 1
        far = OFFSETS[number % 4]

        def one(n, carry, ref=ref, half=half, far=far):
            i, y, c = n >> 2, (n >> 1) & 1, n & 1
            near = offset_of(i)
            dx, dz = jnp.where(half == 0, far, near), jnp.where(half == 0, near, far)
            fetch(ref.at[i, y, c], ((x + dx) & 3) * 2 + y + 8 * half, ((z + dz) & 3) * 2 + c - first_col)
            return carry

        lax.fori_loop(0, 16, one, 0)


def factor_kernel(call, place, *refs):
    start, width = STRIPS[call]
    late = start >= PW // 2
    count = 2 if late else 8
    pieces, refs = refs[:count], refs[count:]
    earlier = refs[: 2 * call]
    out_high, out_low, inv_high, inv_low = refs[2 * call : 4 + 2 * call]
    (lead, high, low, c, diag, inverse, upper, inverse1, low21, load_sem, strip_sem, out_sem) = refs[4 + 2 * call :]
    load_leading(place, pieces, late, lead, load_sem, start // BLK)
    copies = []
    for n in range(call):
        for which, dest in ((0, high), (1, low)):
            copies.append(
                pltpu.make_async_copy(
                    earlier[2 * n + which].at[pl.ds(start - STRIPS[n][0], PW - start), :],
                    dest.at[:, pl.ds(*STRIPS[n])],
                    strip_sem.at[2 * n + which],
                )
            )
    for copy in copies:
        copy.start()

    def wait_lead(n):
        loaded = lead.at[4 * n : 4 * n + 4, PW // 2 if late else 0 :, :]
        pltpu.make_async_copy(loaded, loaded, load_sem.at[n]).wait()

    def outs(kk):
        rows, cols = pl.ds(STEP * kk, PW - start - STEP * kk), pl.ds(STEP * kk, STEP)
        source = pl.ds(start + STEP * kk, STEP)
        return [
            pltpu.make_async_copy(high.at[rows, source], out_high.at[rows, cols], out_sem.at[2 * kk]),
            pltpu.make_async_copy(low.at[rows, source], out_low.at[rows, cols], out_sem.at[2 * kk + 1]),
        ]

    wait_lead(0)
    for copy in copies:
        copy.wait()

    def put(rows, cols, value):
        h, l = split(value)
        high[rows, cols] = h
        low[rows, cols] = l

    def under(at, tile):
        wide = (PW - start - at) // 512

        def one(t, carry):
            tile(pl.multiple_of(at + t * 512, STEP), 512)
            return carry

        lax.fori_loop(0, wide, one, 0)
        if at + wide * 512 < PW - start:
            tile(at + wide * 512, STEP)

    def before(kk):
        if kk and kk % 2 == 0:
            wait_lead(kk // 2)
        known = start + STEP * kk
        r0 = STEP * kk

        def tile(at, size):
            rows = pl.ds(at, size)
            whole = pl.ds(pl.multiple_of(start + at, STEP), size)
            value = jnp.concatenate([lead[2 * kk, whole, :], lead[2 * kk + 1, whole, :]], axis=1)
            if known > 0:
                value = value - pairs(
                    dot_nt, high[rows, :known], low[rows, :known], high[r0 : r0 + STEP, :known], low[r0 : r0 + STEP, :known]
                )
            c[rows, :] = value

        tile(r0, STEP)
        under(r0 + STEP, tile)
        diag[...] = c[r0 : r0 + BLK, :BLK]

    def between(kk):
        r0 = STEP * kk
        col = start + r0
        w1 = inverse[...]
        l21 = near_nt(c[r0 + BLK : r0 + STEP, :BLK], w1)
        diag[...] = c[r0 + BLK : r0 + STEP, BLK:] - near_nt(l21, l21)
        inverse1[...] = w1
        low21[...] = l21
        put(pl.ds(r0, BLK), pl.ds(col, BLK), upper[...].T)
        put(pl.ds(r0, BLK), pl.ds(col + BLK, BLK), jnp.zeros((BLK, BLK), F32))
        put(pl.ds(r0 + BLK, BLK), pl.ds(col, BLK), l21)

    def after(kk):
        r0 = STEP * kk
        col = start + r0
        w2 = inverse[...]
        put(pl.ds(r0 + BLK, BLK), pl.ds(col + BLK, BLK), upper[...].T)
        w21 = -near_nn(w2, near_nn(low21[...], inverse1[...]))
        top = jnp.concatenate([inverse1[...], jnp.zeros((BLK, BLK), F32)], axis=1)
        w = jnp.concatenate([top, jnp.concatenate([w21, w2], axis=1)], axis=0)
        wh, wl = split(w)
        inv_high[kk] = wh
        inv_low[kk] = wl

        def tile(at, size):
            rows = pl.ds(at, size)
            ch, cl = split(c[rows, :])
            put(rows, pl.ds(col, STEP), pairs(dot_nt, ch, cl, inv_high[kk], inv_low[kk]))

        under(r0 + STEP, tile)
        for copy in outs(kk):
            copy.start()

    def half(h, carry):
        for kk in range(width // STEP):
            pl.when(h == 2 * kk)(functools.partial(before, kk))
        w, u = eliminate([diag[8 * i : 8 * i + 8, :] for i in range(16)])
        for i in range(16):
            inverse[8 * i : 8 * i + 8, :] = w[i]
            upper[8 * i : 8 * i + 8, :] = u[i]
        for kk in range(width // STEP):
            pl.when(h == 2 * kk)(functools.partial(between, kk))
            pl.when(h == 2 * kk + 1)(functools.partial(after, kk))
        return carry

    lax.fori_loop(0, width // BLK, half, 0)
    for kk in range(width // STEP):
        for copy in outs(kk):
            copy.wait()


def factor_strip(call, place, pieces, earlier):
    start, width = STRIPS[call]
    rows = PW - start
    known = start + width
    strip = jax.ShapeDtypeStruct((rows, width), BF16)
    inverses = jax.ShapeDtypeStruct((width // STEP, STEP, STEP), BF16)
    block = pltpu.VMEM((BLK, BLK), F32)
    return pl.pallas_call(
        functools.partial(factor_kernel, call),
        out_shape=[strip, strip, inverses, inverses],
        in_specs=[SMEM] + [ANY] * (len(pieces) + 2 * call),
        out_specs=[ANY, ANY, VMEM, VMEM],
        scratch_shapes=[
            pltpu.VMEM((width // BLK, PW, BLK), F32),
            pltpu.VMEM((rows, known), BF16),
            pltpu.VMEM((rows, known), BF16),
            pltpu.VMEM((rows, STEP), F32),
            block,
            block,
            block,
            block,
            block,
            pltpu.SemaphoreType.DMA((width // 512,)),
            pltpu.SemaphoreType.DMA((max(2 * call, 1),)),
            pltpu.SemaphoreType.DMA((2 * width // STEP,)),
        ],
        compiler_params=PARAMS,
        cost_estimate=pl.CostEstimate(flops=int(7e7) * width, bytes_accessed=int(1e8), transcendentals=0),
        name=f"factor{call}",
    )(place, *pieces, *earlier)


def head_kernel(hit, colsel, token, front, f0, f1, g0, g1, own, below, above, opposite, head, late):
    del token
    for n, ref in enumerate((own, below, above, opposite)):
        late[n] = ref[...]
    for w in range(2):
        rows = slice(w * BLK, (w + 1) * BLK)
        for n in range(1, 5):
            total = front[rows, n * BLK : (n + 1) * BLK]
            for k, (first, rest) in enumerate(((f0, g0), (f1, g1))):
                for sel, j in ((1, n), (2, n - 1)):
                    if j < 4:
                        block = first[0, w] if j == 0 else rest[0, w, :, (j - 1) * BLK : j * BLK]
                        use = (hit[k, w] == 1) & (colsel[k, n] == sel)
                        total = total + jnp.where(use, block, F32(0))
            head[rows, (n - 1) * BLK : n * BLK] = total


def head_rows(hit, colsel, token, front, first, rest, late):
    cols = front.shape[1]

    def child(k):
        return lambda i: (4 * k, 0, 0, 0)

    return pl.pallas_call(
        head_kernel,
        grid=(1,),
        out_shape=[
            jax.ShapeDtypeStruct((2 * BLK, cols - BLK), F32),
            jax.ShapeDtypeStruct((4, *late[0].shape), F32),
        ],
        in_specs=[
            SMEM,
            SMEM,
            ANY,
            pl.BlockSpec((2 * BLK, cols), lambda i: (0, 0)),
            pl.BlockSpec((1, 2, BLK, BLK), child(0)),
            pl.BlockSpec((1, 2, BLK, BLK), child(1)),
            pl.BlockSpec((1, 2, BLK, 3 * BLK), child(0)),
            pl.BlockSpec((1, 2, BLK, 3 * BLK), child(1)),
            VMEM,
            VMEM,
            VMEM,
            VMEM,
        ],
        out_specs=[pl.BlockSpec((2 * BLK, cols - BLK), lambda i: (0, 0)), VMEM],
        compiler_params=PARAMS,
        name="head",
    )(hit, colsel, token, front, first, first, rest, rest, *late)


def solve_kernel(place, source, colsel, *refs):
    n_strips = 2 * len(STRIPS)
    strips, inverses, refs = refs[:n_strips], refs[n_strips : 2 * n_strips], refs[2 * n_strips :]
    slabs, refs = refs[:8], refs[8:]
    panel_rows, front, first, rest, panel_out, trailing = refs[:6]
    high, low, xh, xl, yh, yl, raw, yraw, base, child, sems, raw_sem, slab_sem, child_sem = refs[6:]
    x, y, z, core = place[0], place[1], place[2], place[3]
    row = x * 2 + y % 2
    col = (y // 2) * 8 + z * 2 + core
    blocks = PW // STEP
    factor_rows = [[] for _ in range(blocks)]
    for k in range(blocks):
        for n, (start, width) in enumerate(STRIPS):
            if start <= STEP * k:
                cols = min(width, STEP * (k + 1) - start)
                for which, dest in ((0, high), (1, low)):
                    factor_rows[k].append(
                        pltpu.make_async_copy(
                            strips[2 * n + which].at[pl.ds(STEP * k - start, STEP), pl.ds(0, cols)],
                            dest.at[pl.ds(STEP * k, STEP), pl.ds(start, cols)],
                            sems.at[k, 2 * n + which],
                        )
                    )

    def start_all(copies):
        for copy in copies:
            copy.start()

    raws = [pltpu.make_async_copy(panel_rows.at[pl.ds(4 * n, 4)], raw.at[pl.ds(4 * n, 4)], raw_sem.at[n]) for n in range(4)]
    slab_copies = []
    for n, dx in enumerate(SLABS):
        for dl in range(2):
            there = ((x + dx) % 4) * 2 + (y + dl) % 2
            for second in range(2):
                at = pl.multiple_of((there + 8 * second) * BLK, BLK)
                slab_copies.append(
                    pltpu.make_async_copy(
                        slabs[n * 2 + dl].at[pl.ds(second * BLK, BLK), :],
                        yraw.at[pl.ds(at, BLK), :],
                        slab_sem.at[(n * 2 + dl) * 2 + second],
                    )
                )
    children = [
        pltpu.make_async_copy(front.at[2 * BLK :, BLK:], base, child_sem.at[0]),
        pltpu.make_async_copy(first, child.at[:, :, :, pl.ds(0, BLK)], child_sem.at[1]),
        pltpu.make_async_copy(rest, child.at[:, :, :, pl.ds(BLK, 3 * BLK)], child_sem.at[2]),
    ]
    start_all(slab_copies)
    raws[0].start()
    for k in range(3):
        start_all(factor_rows[k])
    for copy in slab_copies:
        copy.wait()
    panel_out[: 2 * BLK, :] = jnp.zeros((2 * BLK, BLK), F32)
    for k in range(PW // STEP):
        known = STEP * k
        if k % 2 == 0:
            raws[k // 2].wait()
            if k // 2 + 1 < len(raws):
                raws[k // 2 + 1].start()
        if k + 3 < blocks:
            start_all(factor_rows[k + 3])
        if k == 5:
            start_all(children)
        for copy in factor_rows[k]:
            copy.wait()
        strip = max(n for n, (start, _) in enumerate(STRIPS) if start <= known)
        wh, wl = inverses[2 * strip], inverses[2 * strip + 1]
        inner = k - STRIPS[strip][0] // STEP
        here = slice(known, known + STEP)
        value = yraw[here, :]
        if k:
            value = value - pairs(dot_nn, high[here, :known], low[here, :known], yh[:known, :], yl[:known, :])
        vh, vl = split(value)
        got = pairs(dot_nn, wh[inner], wl[inner], vh, vl)
        yh[here, :], yl[here, :] = split(got)

        if k % 2 == 0:
            first_inverse = wh[inner], wl[inner]
            continue
        done = known - STEP
        two = slice(done, done + 2 * STEP)
        front_half, back_half = slice(done, known), here

        def tile(t, carry, k=k, done=done, two=two, a=front_half, b=back_half, wa=first_inverse, wb=(wh[inner], wl[inner])):
            rows = pl.ds(pl.multiple_of(t * ROWS, ROWS), ROWS)
            value = jnp.concatenate([raw[2 * k - 2 + n, rows, :] for n in range(4)], axis=1)
            if done:
                value = value - pairs(dot_nt, xh[rows, :done], xl[rows, :done], high[two, :done], low[two, :done])
            xa = pairs(dot_nt, *split(value[:, :STEP]), *wa)
            xah, xal = split(xa)
            vb = value[:, STEP:] - pairs(dot_nt, xah, xal, high[b, a], low[b, a])
            xb = pairs(dot_nt, *split(vb), *wb)
            xh[rows, a], xl[rows, a] = xah, xal
            xh[rows, b], xl[rows, b] = split(xb)
            for side in range(4):

                @pl.when(col == 2 * k - 2 + side)
                def _():
                    got = (xa, xb)[side // 2]
                    at = pl.multiple_of(2 * BLK + t * ROWS, BLK)
                    panel_out[pl.ds(at, ROWS), :] = got[:, (side % 2) * BLK : (side % 2 + 1) * BLK]

            return carry

        lax.fori_loop(0, raw.shape[1] // ROWS, tile, 0)
    lanes = pl.ds(pl.multiple_of(col * BLK, BLK), BLK)
    for second in range(2):
        block_row = row + 8 * second

        @pl.when(block_row >= col)
        def _():
            rows = pl.ds(pl.multiple_of(block_row * BLK, BLK), BLK)
            panel_out[second * BLK : (second + 1) * BLK, :] = high[rows, lanes].astype(F32) + low[rows, lanes].astype(F32)

    trailing[: 2 * BLK, :] = jnp.zeros((2 * BLK, trailing.shape[1]), F32)
    trailing[:, :BLK] = jnp.zeros((trailing.shape[0], BLK), F32)

    for copy in children:
        copy.wait()

    def assemble(q, carry):
        rows = pl.ds(pl.multiple_of(q * BLK, BLK), BLK)
        out = pl.ds(pl.multiple_of((q + 2) * BLK, BLK), BLK)
        for n in range(1, 5):
            total = base[rows, (n - 1) * BLK : n * BLK]
            for k in range(2):
                at = source[k, q + 2]
                use = at >= 0
                at = jnp.maximum(at, 0)
                for sel, j in ((1, n), (2, n - 1)):
                    if j < 4:
                        block = child[at, q & 1, :, j * BLK : (j + 1) * BLK]
                        total = total + jnp.where(use & (colsel[k, n] == sel), block, F32(0))
            trailing[out, n * BLK : (n + 1) * BLK] = total
        return carry

    lax.fori_loop(0, 8, assemble, 0)

    def update(t, carry):
        rows = pl.ds(pl.multiple_of(t * 512, 512), 512)
        out = pl.ds(pl.multiple_of(2 * BLK + t * 512, STEP), 512)
        trailing[out, BLK:] = trailing[out, BLK:] - pairs(dot_nn, xh[rows, :], xl[rows, :], yh[...], yl[...])
        return carry

    lax.fori_loop(0, raw.shape[1] // 512, update, 0)


def solve(place, source, colsel, strips, inverses, slabs, panel_rows, front, first, rest):
    rows, cols = front.shape
    under = rows - 2 * BLK
    return pl.pallas_call(
        solve_kernel,
        out_shape=[jax.ShapeDtypeStruct((rows, BLK), F32), jax.ShapeDtypeStruct((rows, cols), F32)],
        in_specs=[SMEM] * 3 + [ANY] * len(strips) + [VMEM] * len(inverses) + [ANY] * 12,
        out_specs=[VMEM, VMEM],
        scratch_shapes=[
            pltpu.VMEM((PW, PW), BF16),
            pltpu.VMEM((PW, PW), BF16),
            pltpu.VMEM((under, PW), BF16),
            pltpu.VMEM((under, PW), BF16),
            pltpu.VMEM((PW, cols - BLK), BF16),
            pltpu.VMEM((PW, cols - BLK), BF16),
            pltpu.VMEM((16, under, BLK), F32),
            pltpu.VMEM((PW, cols - BLK), F32),
            pltpu.VMEM((under, cols - BLK), F32),
            pltpu.VMEM((8, 2, BLK, 4 * BLK), F32),
            pltpu.SemaphoreType.DMA((PW // STEP, len(strips))),
            pltpu.SemaphoreType.DMA((4,)),
            pltpu.SemaphoreType.DMA((16,)),
            pltpu.SemaphoreType.DMA((3,)),
        ],
        compiler_params=PARAMS,
        name="solve",
    )(place, source, colsel, *strips, *inverses, *slabs, panel_rows, front, first, rest)


def local(front, updates, maps):
    row_at = lax.axis_index("row")
    col_at = lax.axis_index("col")
    place = jnp.stack([row_at // 2, (col_at // 8) * 2 + row_at % 2, (col_at // 2) % 4, col_at % 2]).astype(jnp.int32)
    slots = maps >> 4
    row_slots = lax.dynamic_index_in_dim(slots.reshape(2, 2, 8, 4), row_at, 2, keepdims=False)
    col_slots = lax.dynamic_index_in_dim(slots.reshape(2, 16, 4), col_at, 1, keepdims=False)

    slot = jnp.arange(5)
    own = jnp.pad(row_slots, ((0, 0), (0, 0), (0, 1)), constant_values=-1) == slot
    prior = jnp.pad(row_slots, ((0, 0), (0, 0), (1, 0)), constant_values=-1) == slot
    source = jnp.where(own, slot, jnp.where(prior, slot - 1, -8)) + 4 * jnp.arange(2)[:, None, None]
    source = source.transpose(0, 2, 1).reshape(2, 10).astype(jnp.int32)
    own = jnp.pad(col_slots, ((0, 0), (0, 1)), constant_values=-1) == slot
    prior = jnp.pad(col_slots, ((0, 0), (1, 0)), constant_values=-1) == slot
    colsel = jnp.where(own, 1, jnp.where(prior, 2, 0)).astype(jnp.int32)

    def outgoing(part):
        return part.reshape(2, 8, BLK, part.shape[1]).transpose(1, 0, 2, 3)

    def exchange(outgoing):
        return lax.all_to_all(outgoing, "row", split_axis=0, concat_axis=0, tiled=True)

    first = exchange(outgoing(updates[:, :BLK]))
    meets = col_slots[:, 0] == 0
    panel = front[:, :BLK].reshape(5, 2, BLK, BLK)
    parts = []
    for m in range(5):
        total = panel[m]
        for child in range(2):
            for a in (m, m - 1):
                if 0 <= a < 4:
                    hit = (row_slots[child, :, a] == m) & meets[child]
                    total = total + jnp.where(hit[:, None, None], first[4 * child + a], F32(0))
        parts.append(total)
    corner = parts[0].reshape(2 * BLK, BLK)
    under = jnp.stack(parts[1:]).reshape(8 * BLK, BLK)
    pieces, late = gather_leading(corner, place[1], place[3])

    tokens = [pieces[3][0, 0, 0, 0, 0]]
    panel_rows = lax.all_gather(held(under, tokens), "col", axis=0, tiled=True).reshape(16, 8 * BLK, BLK)
    late = around(held(late, tokens), 2)
    rest = exchange(held(outgoing(updates[:, BLK:]), tokens))

    strips, inverses = [], []

    def factor(call, place, pieces):
        got = factor_strip(call, place, pieces, strips)
        strips.extend(got[:2])
        inverses.extend(got[2:])

    factor(0, place, pieces)
    hit = (row_slots[:, :, 0] == 0).astype(jnp.int32)
    head, late = head_rows(hit, colsel, inverses[0], front, first, rest, late)
    late = [late, move(late, SWAP)]
    slabs = []
    for dx in SLABS:
        for dl in range(2):
            there = [(r, ((r // 2 - dx) % 4) * 2 + (r + dl) % 2) for r in range(8)]
            slabs.append(lax.ppermute(head, "row", there) if dx or dl else head)
    factor(1, place, late)
    factor(2, place, late)
    return tuple(solve(place, source, colsel, strips, inverses, slabs, panel_rows, front, first, rest))


def solution(mesh):
    in_specs = (P("row", "col"), P("row", "col"), P())
    out_specs = (P("row", "col"), P("row", "col"))
    return jax.shard_map(local, mesh=mesh, in_specs=in_specs, out_specs=out_specs, check_vma=False)
```
